32 devices in a mesh: cuts: 4 (over y, core), grid: 8 (over z, x).
Axes of the slice: x: 2, y: 2, z: 4, core: 2. Of those that a mesh axis runs over, the one named last changes fastest.
Arguments:
- orbitals: bfloat16 [32768, 1024], P('grid', 'cuts'), may hold values from -9 to 9, as said below
- potential: float32 [32768], P('grid'), may hold values from -1 to 1
- core_density: float32 [32768], P('grid'), may hold values from 0.05 to 0.5
- occupation: int32 [1024], P('cuts'), may hold values from 0 to 2
- slice_counts: int32 [4], P('cuts'), may hold values from 128 to 256
Outputs:
- orbitals_out: bfloat16 [32768, 1024], P('grid', 'cuts')
- potential_out: float32 [32768], P('grid')
The draws below stay inside these ranges and needn't reach their ends.
Inputs may be any that keep to these rules, and one draw needn't show every extreme that they name: `orbitals`: every entry has magnitude at most 9.
All inputs are finite; a program needn't handle non-finite values.
Results may differ from the reference program's by a relative error of at most 0.0015.
The reference program's roundings to bfloat16 on the way (of `applied` and `rotation`) count: a program that leaves them out, or rounds other values in their place, can miss the bound.
Values may be sent and summed in bfloat16 or wider, within the bound.
A program may use at most 64 MiB of HBM per device.

```python
import math
import jax
import jax.numpy as jnp
from jax import lax

SLICE = 256
STATES = 1024
NG = 32768
N_CUTS = 4


def draw_orbitals(key, part):
    noise = jnp.clip(jax.random.normal(key, (NG, STATES), jnp.float32), -6.0, 6.0)
    mixed = noise + 0.5 * jnp.roll(noise, 1, axis=1)
    return mixed.astype(jnp.bfloat16)


def with_ends(values, rng, smallest, high):
    longest = values.shape.index(max(values.shape))
    spots = []
    for shift in (0, 1):
        where = [jax.random.randint(jax.random.fold_in(rng, axis), (), 0, length) for axis, length in enumerate(values.shape)]
        where[longest] = (where[longest] + shift) % values.shape[longest]
        spots.append(tuple(where))
    return values.at[spots[0]].set(smallest).at[spots[1]].set(high)


def levels(own_key, extent, shards, smallest, high):
    gain, own = 1.0, jax.random.fold_in(own_key, 6)
    for dim, shards_of in shards:
        draws = jnp.exp(jax.random.uniform(jax.random.fold_in(own, dim), (shards_of,), jnp.float32, smallest / len(shards), high / len(shards)))
        gain = gain * jnp.repeat(draws, extent[dim] // shards_of).reshape([-1 if axis == dim else 1 for axis in range(len(extent))])
    return gain


def setup_inputs(seed: int = 0) -> dict:
    splits = jax.random.split(jax.random.key(seed), 6)
    orbitals = draw_orbitals(jax.random.fold_in(splits[5], 71), 0)
    potential = jnp.clip(jax.random.uniform(splits[1], (NG,), jnp.float32, -1.0, 1.0) * levels(splits[1], (NG,), ((0, 8),), -0.4, 0.0), -1.0, 1.0)
    core_density = jnp.clip(jnp.exp(math.log(0.5) - 2.3025851 * jax.random.uniform(splits[2], (NG,), jnp.float32) ** levels(splits[2], (NG,), ((0, 8),), -0.2, 0.2)), 0.05, 0.5)
    occupation = with_ends(jax.random.randint(splits[3], (STATES,), 0, 3), jax.random.fold_in(splits[3], 1), 0, 2).astype(jnp.int32)
    slice_counts = with_ends(jax.random.randint(splits[4], (N_CUTS,), SLICE // 2, SLICE + 1), jax.random.fold_in(splits[4], 1), SLICE // 2, SLICE).astype(jnp.int32)
    return {"orbitals": orbitals, "potential": potential, "core_density": core_density, "occupation": occupation, "slice_counts": slice_counts}


mixing = 0.3
step_size = 0.5

def reference(orbitals, potential, core_density, occupation, slice_counts):
    highest = lax.Precision.HIGHEST
    coefficient = (3.0 / jnp.pi) ** (1.0 / 3.0)
    density = core_density.astype(jnp.float32)
    blocks = []
    for group in range(N_CUTS):
        psi = orbitals[:, group * SLICE:(group + 1) * SLICE]
        wide = psi.astype(jnp.float32)
        kinetic = -0.5 * (jnp.roll(wide, -1, axis=0) + jnp.roll(wide, 1, axis=0) - 2.0 * wide)
        applied = (kinetic + potential[:, None] * wide).astype(jnp.bfloat16)
        intersection = jnp.dot(psi.T.astype(jnp.float32), psi.astype(jnp.float32), preferred_element_type=jnp.float32) / NG
        ritz = jnp.dot(psi.T.astype(jnp.float32), applied.astype(jnp.float32), preferred_element_type=jnp.float32) / NG
        factor = jnp.linalg.cholesky(intersection)
        identity = jnp.eye(SLICE, dtype=jnp.float32)
        inverse = lax.linalg.triangular_solve(factor, identity, left_side=True, lower=True)
        projected = jnp.dot(jnp.dot(inverse, ritz, precision=highest), inverse.T, precision=highest)
        rotation = jnp.dot(inverse.T, identity - step_size * projected, precision=highest).astype(jnp.bfloat16)
        rotated = jnp.dot(psi.astype(jnp.float32), rotation.astype(jnp.float32), preferred_element_type=jnp.float32)
        blocks.append(rotated.astype(jnp.bfloat16))
        live = (jnp.arange(SLICE) < slice_counts[group]).astype(jnp.float32)
        weights = occupation[group * SLICE:(group + 1) * SLICE].astype(jnp.float32) * live / (2.0 * STATES)
        density = density + jnp.sum(rotated * rotated * weights[None, :], axis=1)
    potential_out = (1.0 - mixing) * potential + mixing * (-coefficient * jnp.cbrt(density))
    return (jnp.concatenate(blocks, axis=1), potential_out)
```

```python
import functools

import jax
import jax.numpy as jnp
from jax import lax
from jax.experimental import pallas as pl
from jax.experimental.pallas import tpu as pltpu
from jax.sharding import PartitionSpec as P

mixing = 0.3
step_size = 0.5
lanes = 128
halo = 16
block = 32
panel = 8
columns = (((0,), (0,)), ((), ()))
across = (((1,), (1,)), ((), ()))
highest = lax.Precision.HIGHEST


def three_parts(x):
    high = x.astype(jnp.bfloat16)
    rest = x - high.astype(jnp.float32)
    middle = rest.astype(jnp.bfloat16)
    low = (rest - middle.astype(jnp.float32)).astype(jnp.bfloat16)
    return high, middle, low


def eliminate(left, right):
    size = left.shape[0]
    rows = lax.broadcasted_iota(jnp.int32, (size, lanes), 0)
    tiles = [left[:, i : i + lanes] for i in range(0, left.shape[1], lanes)]
    tiles += [right[:, i : i + lanes] for i in range(0, right.shape[1], lanes)]
    for first in range(0, size, panel):
        spread = [
            jnp.broadcast_to(tiles[0][:, c : c + 1], (size, lanes))
            for c in range(first, first + panel)
        ]
        for step in range(panel):
            j = first + step
            column = spread[step]
            factor = column * (1.0 / column[j : j + 1, :])
            factor = jnp.where(rows > j, factor, 0.0)
            for c in range(step + 1, panel):
                spread[c] = spread[c] - factor * spread[c][j : j + 1, :]
            tiles = [t - factor * t[j : j + 1, :] for t in tiles]
    at = lax.broadcasted_iota(jnp.int32, (size, lanes), 1)
    pivots = jnp.sum(jnp.where(rows == at, tiles[0], 0.0), axis=1, keepdims=True)
    scale = lax.rsqrt(pivots)
    scale = scale * (1.5 - 0.5 * pivots * scale * scale)
    tiles = [t * scale for t in tiles]
    half = left.shape[1] // lanes
    return jnp.concatenate(tiles[:half], axis=1), jnp.concatenate(tiles[half:], axis=1)


def kernel(
    groups,
    slices,
    psi_hbm,
    potential_ref,
    occupation_ref,
    count_ref,
    rotation_ref,
    density_ref,
    psi,
    applied,
    gram,
    landed,
    summed,
    work,
    inverse_ref,
    mine,
    shares,
    load_sem,
    halo_send,
    halo_recv,
    scatter_send,
    scatter_recv,
    gather_send,
    gather_recv,
    share_send,
    share_recv,
):
    points, width = psi_hbm.shape
    me = lax.axis_index("grid")
    cut = lax.axis_index("cuts")
    part = width // groups
    chunk = lanes * 8
    total_points = points * groups

    load = pltpu.make_async_copy(psi_hbm, psi.at[pl.ds(halo, points)], load_sem)
    load.start()
    barrier = pltpu.get_barrier_semaphore()
    for d in range(1, groups):
        pl.semaphore_signal(
            barrier, inc=1, device_id={"grid": lax.rem(me + d, groups)}, device_id_type=pl.DeviceIdType.MESH
        )
    for d in range(1, slices):
        pl.semaphore_signal(
            barrier, inc=1, device_id={"cuts": lax.rem(cut + d, slices)}, device_id_type=pl.DeviceIdType.MESH
        )
    load.wait()

    gram[0] = jnp.zeros((width, width), jnp.float32)
    gram[1] = jnp.zeros((width, width), jnp.float32)

    def overlap(i, carry):
        x = psi[pl.ds(pl.multiple_of(i * chunk, chunk) + halo, chunk), :]
        gram[0] += lax.dot_general(x, x, columns, preferred_element_type=jnp.float32)
        return carry

    lax.fori_loop(0, points // chunk, overlap, 0)
    pl.semaphore_wait(barrier, groups + slices - 2)

    up = pltpu.make_async_remote_copy(
        src_ref=psi_hbm.at[pl.ds(points - halo, halo)],
        dst_ref=psi.at[pl.ds(0, halo)],
        send_sem=halo_send.at[0],
        recv_sem=halo_recv.at[0],
        device_id={"grid": lax.rem(me + 1, groups)},
        device_id_type=pl.DeviceIdType.MESH,
    )
    down = pltpu.make_async_remote_copy(
        src_ref=psi_hbm.at[pl.ds(0, halo)],
        dst_ref=psi.at[pl.ds(points + halo, halo)],
        send_sem=halo_send.at[1],
        recv_sem=halo_recv.at[1],
        device_id={"grid": lax.rem(me + groups - 1, groups)},
        device_id_type=pl.DeviceIdType.MESH,
    )
    up.start()
    down.start()

    own = pl.ds(pl.multiple_of(me * part, part), part)

    def scatter(which):
        copies = []
        for d in range(1, groups):
            to = lax.rem(me + d, groups)
            copies.append(
                pltpu.make_async_remote_copy(
                    src_ref=gram.at[which, pl.ds(pl.multiple_of(to * part, part), part)],
                    dst_ref=landed.at[which, d - 1],
                    send_sem=scatter_send.at[which, d - 1],
                    recv_sem=scatter_recv.at[which, d - 1],
                    device_id={"grid": to},
                    device_id_type=pl.DeviceIdType.MESH,
                )
            )
        for copy in copies:
            copy.start()
        return copies

    def gather(which, copies):
        for copy in copies:
            copy.wait()
        total = gram[which, own, :]
        for d in range(groups - 1):
            total = total + landed[which, d]
        summed[which, own, :] = total * (1.0 / total_points)
        copies = []
        for d in range(1, groups):
            copies.append(
                pltpu.make_async_remote_copy(
                    src_ref=summed.at[which, own],
                    dst_ref=summed.at[which, own],
                    send_sem=gather_send.at[which, d - 1],
                    recv_sem=gather_recv.at[which, d - 1],
                    device_id={"grid": lax.rem(me + d, groups)},
                    device_id_type=pl.DeviceIdType.MESH,
                )
            )
        for copy in copies:
            copy.start()
        return copies

    first = scatter(0)
    up.wait()
    down.wait()

    def ritz(i, carry):
        base = pl.multiple_of(i * chunk, chunk)
        values = potential_ref[pl.ds(pl.multiple_of(i * 8, 8), 8), :]
        for s in range(8):
            x = psi[pl.ds(base + s * lanes, lanes + 2 * halo), :].astype(jnp.float32)
            middle = x[halo : halo + lanes]
            before = x[halo - 1 : halo + lanes - 1]
            after = x[halo + 1 : halo + lanes + 1]
            local = jnp.broadcast_to(values[s : s + 1, :], (lanes, lanes)).T
            local = jnp.concatenate([local] * (width // lanes), axis=1)
            kinetic = -0.5 * (after + before - 2.0 * middle)
            applied[s * lanes : (s + 1) * lanes, :] = (kinetic + local * middle).astype(jnp.bfloat16)
        x = psi[pl.ds(base + halo, chunk), :]
        gram[1] += lax.dot_general(x, applied[...], columns, preferred_element_type=jnp.float32)
        return carry

    lax.fori_loop(0, points // chunk, ritz, 0)
    first = gather(0, first)
    second = scatter(1)

    row = lax.broadcasted_iota(jnp.int32, (width, width), 0)
    column = lax.broadcasted_iota(jnp.int32, (width, width), 1)
    identity = (row == column).astype(jnp.float32)
    for copy in first:
        copy.wait()
    work[:, :width] = summed[0]
    work[:, width:] = identity

    def factor(k, carry):
        here = pl.ds(pl.multiple_of(k * block, block), block)
        back = lax.rem(width - k * block, width)
        left = pltpu.roll(work[here, :width], back, 1)
        left, right = eliminate(left, work[here, width:])
        inverse_ref[here, :] = right
        left = pltpu.roll(left, k * block, 1)
        at = lax.broadcasted_iota(jnp.int32, (block, width), 1)
        left = jnp.where(at >= (k + 1) * block, left, 0.0)
        lh, lm, ll = three_parts(left)
        rh, rm, rl = three_parts(right)
        lhs = jnp.concatenate([lh, lh, lm, lh, ll, lm], axis=0)
        a = jnp.concatenate([lh, lm, lh, ll, lh, lm], axis=0)
        b = jnp.concatenate([rh, rm, rh, rl, rh, rm], axis=0)
        rhs = jnp.concatenate([a, b], axis=1)
        work[...] -= lax.dot_general(lhs, rhs, columns, preferred_element_type=jnp.float32)
        return carry

    blocks = width // block
    lax.fori_loop(0, blocks // 2, factor, 0)
    second = gather(1, second)
    lax.fori_loop(blocks // 2, blocks, factor, 0)
    for copy in second:
        copy.wait()

    inverse = inverse_ref[...]
    projected = jnp.dot(inverse, summed[1], precision=highest, preferred_element_type=jnp.float32)
    projected = lax.dot_general(
        projected, inverse, across, precision=highest, preferred_element_type=jnp.float32
    )
    rotation = lax.dot_general(
        inverse,
        identity - step_size * projected,
        columns,
        precision=highest,
        preferred_element_type=jnp.float32,
    ).astype(jnp.bfloat16)
    rotation_ref[...] = rotation

    state = lax.broadcasted_iota(jnp.int32, (1, width), 1)
    live = (state < count_ref[0]).astype(jnp.float32)
    weights = occupation_ref[...].astype(jnp.float32) * live / (2.0 * width * slices)

    def contribute(i, carry):
        x = psi[pl.ds(pl.multiple_of(i * chunk, chunk) + halo, chunk), :]
        rotated = jnp.dot(x, rotation_ref[...], preferred_element_type=jnp.float32)
        square = rotated * rotated * weights
        narrow = square[:, :lanes]
        for c in range(lanes, width, lanes):
            narrow = narrow + square[:, c : c + lanes]
        sums = [
            jnp.sum(narrow[s * lanes : (s + 1) * lanes].T, axis=0, keepdims=True) for s in range(8)
        ]
        mine[pl.ds(pl.multiple_of(i * 8, 8), 8), :] = jnp.concatenate(sums, axis=0)
        return carry

    lax.fori_loop(0, points // chunk, contribute, 0)
    copies = []
    for d in range(1, slices):
        copies.append(
            pltpu.make_async_remote_copy(
                src_ref=mine,
                dst_ref=shares.at[cut],
                send_sem=share_send.at[d - 1],
                recv_sem=share_recv.at[d - 1],
                device_id={"cuts": lax.rem(cut + d, slices)},
                device_id_type=pl.DeviceIdType.MESH,
            )
        )
    for copy in copies:
        copy.start()
    shares[cut] = mine[...]
    for copy in copies:
        copy.wait()
    total = shares[0]
    for c in range(1, slices):
        total = total + shares[c]
    density_ref[...] = total


def per_device(orbitals, potential, core_density, occupation, slice_counts):
    coefficient = (3.0 / jnp.pi) ** (1.0 / 3.0)
    points, width = orbitals.shape
    groups, slices = (lax.axis_size("grid"), lax.axis_size("cuts"))
    folded = (points // lanes, lanes)
    part = width // groups
    vmem = pl.BlockSpec(memory_space=pltpu.VMEM)
    rotation, contribution = pl.pallas_call(
        functools.partial(kernel, groups, slices),
        out_shape=(
            jax.ShapeDtypeStruct((width, width), jnp.bfloat16),
            jax.ShapeDtypeStruct(folded, jnp.float32),
        ),
        in_specs=[
            pl.BlockSpec(memory_space=pl.ANY),
            vmem,
            vmem,
            pl.BlockSpec(memory_space=pltpu.SMEM),
        ],
        out_specs=(vmem, vmem),
        scratch_shapes=[
            pltpu.VMEM((points + 2 * halo, width), jnp.bfloat16),
            pltpu.VMEM((8 * lanes, width), jnp.bfloat16),
            pltpu.VMEM((2, width, width), jnp.float32),
            pltpu.VMEM((2, groups - 1, part, width), jnp.float32),
            pltpu.VMEM((2, width, width), jnp.float32),
            pltpu.VMEM((width, 2 * width), jnp.float32),
            pltpu.VMEM((width, width), jnp.float32),
            pltpu.VMEM(folded, jnp.float32),
            pltpu.VMEM((slices,) + folded, jnp.float32),
            pltpu.SemaphoreType.DMA,
            pltpu.SemaphoreType.DMA((2,)),
            pltpu.SemaphoreType.DMA((2,)),
            pltpu.SemaphoreType.DMA((2, groups - 1)),
            pltpu.SemaphoreType.DMA((2, groups - 1)),
            pltpu.SemaphoreType.DMA((2, groups - 1)),
            pltpu.SemaphoreType.DMA((2, groups - 1)),
            pltpu.SemaphoreType.DMA((slices - 1,)),
            pltpu.SemaphoreType.DMA((slices - 1,)),
        ],
        compiler_params=pltpu.CompilerParams(
            collective_id=0, has_side_effects=True, vmem_limit_bytes=40 * 1024 * 1024
        ),
        cost_estimate=pl.CostEstimate(
            flops=8 * points * width * width, bytes_accessed=2 * points * width, transcendentals=0
        ),
    )(orbitals, potential.reshape(folded), occupation.reshape(1, width), slice_counts)
    rotated = jnp.dot(orbitals, rotation, preferred_element_type=jnp.float32)
    orbitals_out = rotated.astype(jnp.bfloat16)
    density = core_density + contribution.reshape(points)
    potential_out = (1.0 - mixing) * potential + mixing * (-coefficient * jnp.cbrt(density))
    return (orbitals_out, potential_out)


def solution(mesh):
    placed = (P("grid", "cuts"), P("grid"), P("grid"), P("cuts"), P("cuts"))
    return jax.shard_map(
        per_device,
        mesh=mesh,
        in_specs=placed,
        out_specs=(P("grid", "cuts"), P("grid")),
        check_vma=False,
    )
```

```python
import functools
import math

import jax
import jax.numpy as jnp
from jax import lax
from jax.experimental import pallas as pl
from jax.experimental.pallas import tpu as pltpu
from jax.sharding import PartitionSpec as P

mixing = 0.3
step_size = 0.5
lanes = 128
halo = 16
block = 32
panel = 8
columns = (((0,), (0,)), ((), ()))
across = (((1,), (1,)), ((), ()))
highest = lax.Precision.HIGHEST


def three_parts(x):
    high = x.astype(jnp.bfloat16)
    rest = x - high.astype(jnp.float32)
    middle = rest.astype(jnp.bfloat16)
    low = (rest - middle.astype(jnp.float32)).astype(jnp.bfloat16)
    return high, middle, low


def spread_rows(tile, r):
    return jnp.broadcast_to(tile[r : r + 1, :], tile.shape)


def eliminate(rows):
    size, width = rows.shape
    shape = (panel, lanes)
    sub = lax.broadcasted_iota(jnp.int32, shape, 0)
    at = lax.broadcasted_iota(jnp.int32, shape, 1)
    count = size // panel
    tiles = []
    for g in range(count):
        group = rows[g * panel : (g + 1) * panel]
        tiles.append([group[:, i : i + lanes] for i in range(0, width, lanes)])
        tiles[g].append((at == sub + g * panel).astype(jnp.float32))
    done = []
    for p in range(count):
        below = range(p + 1, count)
        spread = {
            (g, c): jnp.broadcast_to(tiles[g][0][:, p * panel + c : p * panel + c + 1], shape)
            for g in range(p, count)
            for c in range(panel)
        }
        pivot = {(r, c): spread_rows(spread[p, c], r) for r in range(panel) for c in range(r + 1)}
        lines = [[spread_rows(t, r) for t in tiles[p]] for r in range(panel)]
        factors = {}
        for j in range(panel):
            inverse = 1.0 / pivot[j, j]
            for r in range(j + 1, panel):
                ratio = pivot[r, j] * inverse
                for c in range(j + 1, r + 1):
                    pivot[r, c] = pivot[r, c] - ratio * pivot[c, j]
                lines[r] = [x - ratio * y for x, y in zip(lines[r], lines[j])]
            for g in below:
                factors[g, j] = spread[g, j] * inverse
                for c in range(j + 1, panel):
                    spread[g, c] = spread[g, c] - factors[g, j] * pivot[c, j]
        for g in below:
            for t in range(len(tiles[g])):
                terms = [factors[g, j] * lines[j][t] for j in range(panel)]
                while len(terms) > 1:
                    terms = [x + y for x, y in zip(terms[::2], terms[1::2])]
                tiles[g][t] = tiles[g][t] - terms[0]
        scaled = []
        for r in range(panel):
            root = lax.rsqrt(pivot[r, r])
            root = root * (1.5 - 0.5 * (pivot[r, r] * root) * root)
            scaled.append([x * root for x in lines[r]])
        merged = scaled[0]
        for r in range(1, panel):
            merged = [jnp.where(sub == r, x, y) for x, y in zip(scaled[r], merged)]
        done.append(merged)
    stack = [jnp.concatenate([group[t] for group in done], axis=0) for t in range(len(done[0]))]
    return jnp.concatenate(stack[:-1], axis=1), stack[-1]


def kernel(
    groups,
    slices,
    psi_hbm,
    potential_hbm,
    occupation_hbm,
    count_ref,
    rotation_ref,
    density_ref,
    psi,
    potential_ref,
    occupation_ref,
    applied,
    full,
    gram,
    landed,
    summed,
    work,
    inverse_ref,
    mine,
    shares,
    load_sem,
    small_sem,
    halo_send,
    halo_recv,
    scatter_send,
    scatter_recv,
    gather_send,
    gather_recv,
    share_send,
    share_recv,
):
    points, width = psi_hbm.shape
    me = lax.axis_index("grid")
    cut = lax.axis_index("cuts")
    corner = width // 2
    small_split = width % (2 * lanes) == 0 and (3 * width // 4) % (8 * groups) == 0
    packed = 3 * width // 4 if small_split else width
    parts = (packed // groups, width // groups)
    chunk = lanes * 8
    total_points = points * groups

    load = pltpu.make_async_copy(psi_hbm, psi.at[pl.ds(halo, points)], load_sem)
    load.start()
    small = [
        pltpu.make_async_copy(potential_hbm, potential_ref, small_sem.at[0]),
        pltpu.make_async_copy(occupation_hbm, occupation_ref, small_sem.at[1]),
    ]
    for copy in small:
        copy.start()
    barrier = pltpu.get_barrier_semaphore()
    for d in range(1, groups):
        pl.semaphore_signal(
            barrier, inc=1, device_id={"grid": lax.rem(me + d, groups)}, device_id_type=pl.DeviceIdType.MESH
        )
    for d in range(1, slices):
        pl.semaphore_signal(
            barrier, inc=1, device_id={"cuts": lax.rem(cut + d, slices)}, device_id_type=pl.DeviceIdType.MESH
        )
    load.wait()

    full[...] = jnp.zeros((width, width), jnp.float32)
    gram[1] = jnp.zeros((width, width), jnp.float32)

    def overlap(i, carry):
        x = psi[pl.ds(pl.multiple_of(i * chunk, chunk) + halo, chunk), :]
        full[...] += lax.dot_general(x, x, columns, preferred_element_type=jnp.float32)
        return carry

    lax.fori_loop(0, points // chunk, overlap, 0)
    if small_split:
        gram[0, :corner, :] = full[:corner, :]
        gram[0, corner:packed, :corner] = full[corner:packed, corner:]
        gram[0, corner:packed, corner:] = full[packed:, corner:]
    else:
        gram[0] = full[...]
    pl.semaphore_wait(barrier, groups + slices - 2)

    up = pltpu.make_async_remote_copy(
        src_ref=psi_hbm.at[pl.ds(points - halo, halo)],
        dst_ref=psi.at[pl.ds(0, halo)],
        send_sem=halo_send.at[0],
        recv_sem=halo_recv.at[0],
        device_id={"grid": lax.rem(me + 1, groups)},
        device_id_type=pl.DeviceIdType.MESH,
    )
    down = pltpu.make_async_remote_copy(
        src_ref=psi_hbm.at[pl.ds(0, halo)],
        dst_ref=psi.at[pl.ds(points + halo, halo)],
        send_sem=halo_send.at[1],
        recv_sem=halo_recv.at[1],
        device_id={"grid": lax.rem(me + groups - 1, groups)},
        device_id_type=pl.DeviceIdType.MESH,
    )
    up.start()
    down.start()

    def scatter(which):
        part = parts[which]
        copies = []
        for d in range(1, groups):
            to = lax.rem(me + d, groups)
            copies.append(
                pltpu.make_async_remote_copy(
                    src_ref=gram.at[which, pl.ds(pl.multiple_of(to * part, part), part)],
                    dst_ref=landed.at[which, d - 1, pl.ds(0, part)],
                    send_sem=scatter_send.at[which, d - 1],
                    recv_sem=scatter_recv.at[which, d - 1],
                    device_id={"grid": to},
                    device_id_type=pl.DeviceIdType.MESH,
                )
            )
        for copy in copies:
            copy.start()
        return copies

    def gather(which, copies):
        part = parts[which]
        own = pl.ds(pl.multiple_of(me * part, part), part)
        for copy in copies:
            copy.wait()
        total = gram[which, own, :]
        for d in range(groups - 1):
            total = total + landed[which, d, :part, :]
        summed[which, own, :] = total * (1.0 / total_points)
        copies = []
        for d in range(1, groups):
            copies.append(
                pltpu.make_async_remote_copy(
                    src_ref=summed.at[which, own],
                    dst_ref=summed.at[which, own],
                    send_sem=gather_send.at[which, d - 1],
                    recv_sem=gather_recv.at[which, d - 1],
                    device_id={"grid": lax.rem(me + d, groups)},
                    device_id_type=pl.DeviceIdType.MESH,
                )
            )
        for copy in copies:
            copy.start()
        return copies

    first = scatter(0)
    up.wait()
    down.wait()
    for copy in small:
        copy.wait()

    def ritz(i, carry):
        base = pl.multiple_of(i * chunk, chunk)
        values = potential_ref[pl.ds(pl.multiple_of(i * 8, 8), 8), :]
        for s in range(8):
            x = psi[pl.ds(base + s * lanes, lanes + 2 * halo), :].astype(jnp.float32)
            middle = x[halo : halo + lanes]
            before = x[halo - 1 : halo + lanes - 1]
            after = x[halo + 1 : halo + lanes + 1]
            local = jnp.broadcast_to(values[s : s + 1, :], (lanes, lanes)).T
            local = jnp.concatenate([local] * (width // lanes), axis=1)
            kinetic = -0.5 * (after + before - 2.0 * middle)
            applied[s * lanes : (s + 1) * lanes, :] = (kinetic + local * middle).astype(jnp.bfloat16)
        x = psi[pl.ds(base + halo, chunk), :]
        gram[1] += lax.dot_general(x, applied[...], columns, preferred_element_type=jnp.float32)
        return carry

    lax.fori_loop(0, points // chunk, ritz, 0)
    first = gather(0, first)
    second = scatter(1)

    row = lax.broadcasted_iota(jnp.int32, (width, width), 0)
    column = lax.broadcasted_iota(jnp.int32, (width, width), 1)
    identity = (row == column).astype(jnp.float32)
    for copy in first:
        copy.wait()
    if small_split:
        work[:corner, :] = summed[0, :corner, :]
        work[corner:, :corner] = jnp.zeros((width - corner, corner), jnp.float32)
        work[corner:packed, corner:] = summed[0, corner:packed, :corner]
        work[packed:, corner:] = summed[0, corner:packed, corner:]
    else:
        work[...] = summed[0]

    def factor(k, carry):
        here = pl.ds(pl.multiple_of(k * block, block), block)
        rows, own_inverse = eliminate(pltpu.roll(work[here, :], lax.rem(width - k * block, width), 1))
        at = lax.broadcasted_iota(jnp.int32, (block, width), 1)
        wide = jnp.concatenate([own_inverse] * (width // lanes), axis=1)
        solved = pltpu.roll(jnp.where(at < block, wide, rows), k * block, 1)
        ahead = jnp.where(at >= (k + 1) * block, solved, 0.0)
        inverse_ref[here, :] = jnp.where(at >= (k + 1) * block, 0.0, solved)
        ah, am, al = three_parts(ahead)
        sh, sm, sl = three_parts(solved)
        lhs = jnp.concatenate([ah, ah, am, ah, al, am], axis=0)
        rhs = jnp.concatenate([sh, sm, sh, sl, sh, sm], axis=0)
        update = lax.dot_general(lhs, rhs, columns, preferred_element_type=jnp.float32)
        kept = (column < k * block) | (column >= (k + 1) * block)
        work[...] = jnp.where(kept, work[...], 0.0) - update
        return carry

    blocks = width // block
    lax.fori_loop(0, blocks // 2, factor, 0)
    second = gather(1, second)
    lax.fori_loop(blocks // 2, blocks, factor, 0)
    for copy in second:
        copy.wait()

    inverse = inverse_ref[...]
    projected = jnp.dot(inverse, summed[1], precision=highest, preferred_element_type=jnp.float32)
    projected = lax.dot_general(
        projected, inverse, across, precision=highest, preferred_element_type=jnp.float32
    )
    rotation = lax.dot_general(
        inverse,
        identity - step_size * projected,
        columns,
        precision=highest,
        preferred_element_type=jnp.float32,
    ).astype(jnp.bfloat16)
    rotation_ref[...] = rotation

    state = lax.broadcasted_iota(jnp.int32, (1, width), 1)
    live = (state < count_ref[0]).astype(jnp.float32)
    weights = occupation_ref[...].astype(jnp.float32) * live / (2.0 * width * slices)

    def contribute(i, carry):
        x = psi[pl.ds(pl.multiple_of(i * chunk, chunk) + halo, chunk), :]
        rotated = jnp.dot(x, rotation_ref[...], preferred_element_type=jnp.float32)
        square = rotated * rotated * weights
        narrow = square[:, :lanes]
        for c in range(lanes, width, lanes):
            narrow = narrow + square[:, c : c + lanes]
        sums = [
            jnp.sum(narrow[s * lanes : (s + 1) * lanes].T, axis=0, keepdims=True) for s in range(8)
        ]
        mine[pl.ds(pl.multiple_of(i * 8, 8), 8), :] = jnp.concatenate(sums, axis=0)
        return carry

    lax.fori_loop(0, points // chunk, contribute, 0)
    copies = []
    for d in range(1, slices):
        copies.append(
            pltpu.make_async_remote_copy(
                src_ref=mine,
                dst_ref=shares.at[cut],
                send_sem=share_send.at[d - 1],
                recv_sem=share_recv.at[d - 1],
                device_id={"cuts": lax.rem(cut + d, slices)},
                device_id_type=pl.DeviceIdType.MESH,
            )
        )
    for copy in copies:
        copy.start()
    shares[cut] = mine[...]
    for copy in copies:
        copy.wait()
    total = shares[0]
    for c in range(1, slices):
        total = total + shares[c]
    density_ref[...] = total


def finish(psi_ref, rotation_ref, contribution_ref, core_ref, potential_ref, out_ref, mixed_ref):
    coefficient = (3.0 / math.pi) ** (1.0 / 3.0)
    rotated = jnp.dot(psi_ref[...], rotation_ref[...], preferred_element_type=jnp.float32)
    out_ref[...] = rotated.astype(jnp.bfloat16)
    root = jnp.exp(jnp.log(core_ref[...] + contribution_ref[...]) * (1.0 / 3.0))
    mixed_ref[...] = (1.0 - mixing) * potential_ref[...] + mixing * (-coefficient * root)


def per_device(orbitals, potential, core_density, occupation, slice_counts):
    points, width = orbitals.shape
    groups, slices = (lax.axis_size("grid"), lax.axis_size("cuts"))
    folded = (points // lanes, lanes)
    part = width // groups
    vmem = pl.BlockSpec(memory_space=pltpu.VMEM)
    rotation, contribution = pl.pallas_call(
        functools.partial(kernel, groups, slices),
        out_shape=(
            jax.ShapeDtypeStruct((width, width), jnp.bfloat16),
            jax.ShapeDtypeStruct(folded, jnp.float32),
        ),
        in_specs=[
            pl.BlockSpec(memory_space=pltpu.HBM),
            pl.BlockSpec(memory_space=pltpu.HBM),
            pl.BlockSpec(memory_space=pltpu.HBM),
            pl.BlockSpec(memory_space=pltpu.SMEM),
        ],
        out_specs=(vmem, vmem),
        scratch_shapes=[
            pltpu.VMEM((points + 2 * halo, width), jnp.bfloat16),
            pltpu.VMEM(folded, jnp.float32),
            pltpu.VMEM((1, width), jnp.int32),
            pltpu.VMEM((8 * lanes, width), jnp.bfloat16),
            pltpu.VMEM((width, width), jnp.float32),
            pltpu.VMEM((2, width, width), jnp.float32),
            pltpu.VMEM((2, groups - 1, part, width), jnp.float32),
            pltpu.VMEM((2, width, width), jnp.float32),
            pltpu.VMEM((width, width), jnp.float32),
            pltpu.VMEM((width, width), jnp.float32),
            pltpu.VMEM(folded, jnp.float32),
            pltpu.VMEM((slices,) + folded, jnp.float32),
            pltpu.SemaphoreType.DMA,
            pltpu.SemaphoreType.DMA((2,)),
            pltpu.SemaphoreType.DMA((2,)),
            pltpu.SemaphoreType.DMA((2,)),
            pltpu.SemaphoreType.DMA((2, groups - 1)),
            pltpu.SemaphoreType.DMA((2, groups - 1)),
            pltpu.SemaphoreType.DMA((2, groups - 1)),
            pltpu.SemaphoreType.DMA((2, groups - 1)),
            pltpu.SemaphoreType.DMA((slices - 1,)),
            pltpu.SemaphoreType.DMA((slices - 1,)),
        ],
        compiler_params=pltpu.CompilerParams(
            collective_id=0, has_side_effects=True, vmem_limit_bytes=40 * 1024 * 1024
        ),
        cost_estimate=pl.CostEstimate(
            flops=8 * points * width * width, bytes_accessed=2 * points * width, transcendentals=0
        ),
    )(orbitals, potential.reshape(folded), occupation.reshape(1, width), slice_counts)
    chunk = 8 * lanes
    tall = pl.BlockSpec((chunk, width), lambda i: (i, 0))
    flat = pl.BlockSpec((8, lanes), lambda i: (i, 0))
    orbitals_out, potential_out = pl.pallas_call(
        finish,
        grid=(points // chunk,),
        out_shape=(
            jax.ShapeDtypeStruct((points, width), jnp.bfloat16),
            jax.ShapeDtypeStruct(folded, jnp.float32),
        ),
        in_specs=[tall, pl.BlockSpec((width, width), lambda i: (0, 0)), flat, flat, flat],
        out_specs=(tall, flat),
        cost_estimate=pl.CostEstimate(
            flops=2 * points * width * width, bytes_accessed=4 * points * width, transcendentals=0
        ),
    )(orbitals, rotation, contribution, core_density.reshape(folded), potential.reshape(folded))
    return (orbitals_out, potential_out.reshape(points))


def solution(mesh):
    placed = (P("grid", "cuts"), P("grid"), P("grid"), P("cuts"), P("cuts"))
    return jax.shard_map(
        per_device,
        mesh=mesh,
        in_specs=placed,
        out_specs=(P("grid", "cuts"), P("grid")),
        check_vma=False,
    )
```

```python
import functools
import math

import jax
import jax.numpy as jnp
from jax import lax
from jax.experimental import pallas as pl
from jax.experimental.pallas import tpu as pltpu
from jax.sharding import PartitionSpec as P

mixing = 0.3
step_size = 0.5
lanes = 128
halo = 16
block = 32
panel = 8
columns = (((0,), (0,)), ((), ()))
across = (((1,), (1,)), ((), ()))
highest = lax.Precision.HIGHEST


def three_parts(x):
    high = x.astype(jnp.bfloat16)
    rest = x - high.astype(jnp.float32)
    middle = rest.astype(jnp.bfloat16)
    low = (rest - middle.astype(jnp.float32)).astype(jnp.bfloat16)
    return high, middle, low


def spread_rows(tile, r):
    return jnp.broadcast_to(tile[r : r + 1, :], tile.shape)


def eliminate(rows):
    size, width = rows.shape
    shape = (panel, lanes)
    sub = lax.broadcasted_iota(jnp.int32, shape, 0)
    at = lax.broadcasted_iota(jnp.int32, shape, 1)
    count = size // panel
    tiles = []
    for g in range(count):
        group = rows[g * panel : (g + 1) * panel]
        tiles.append([group[:, i : i + lanes] for i in range(0, width, lanes)])
        tiles[g].append((at == sub + g * panel).astype(jnp.float32))
    done = []
    for p in range(count):
        below = range(p + 1, count)
        spread = {
            (g, c): jnp.broadcast_to(tiles[g][0][:, p * panel + c : p * panel + c + 1], shape)
            for g in range(p, count)
            for c in range(panel)
        }
        pivot = {(r, c): spread_rows(spread[p, c], r) for r in range(panel) for c in range(r + 1)}
        lines = [[spread_rows(t, r) for t in tiles[p]] for r in range(panel)]
        factors = {}
        for j in range(panel):
            inverse = pltpu.reciprocal(pivot[j, j], approx=True)
            for r in range(j + 1, panel):
                ratio = pivot[r, j] * inverse
                for c in range(j + 1, r + 1):
                    pivot[r, c] = pivot[r, c] - (pivot[r, j] * pivot[c, j]) * inverse
                lines[r] = [x - ratio * y for x, y in zip(lines[r], lines[j])]
            for g in below:
                factors[g, j] = spread[g, j] * inverse
                for c in range(j + 1, panel):
                    spread[g, c] = spread[g, c] - factors[g, j] * pivot[c, j]
        for g in below:
            for t in range(len(tiles[g])):
                terms = [factors[g, j] * lines[j][t] for j in range(panel)]
                while len(terms) > 1:
                    terms = [x + y for x, y in zip(terms[::2], terms[1::2])]
                tiles[g][t] = tiles[g][t] - terms[0]
        scaled = []
        for r in range(panel):
            root = lax.rsqrt(pivot[r, r])
            scaled.append([x * root for x in lines[r]])
        merged = scaled[0]
        for r in range(1, panel):
            merged = [jnp.where(sub == r, x, y) for x, y in zip(scaled[r], merged)]
        done.append(merged)
    stack = [jnp.concatenate([group[t] for group in done], axis=0) for t in range(len(done[0]))]
    return jnp.concatenate(stack[:-1], axis=1), stack[-1]


def kernel(
    groups,
    slices,
    psi_hbm,
    potential_hbm,
    core_hbm,
    occupation_hbm,
    count_ref,
    out_hbm,
    mixed_ref,
    psi,
    potential_ref,
    core_ref,
    occupation_ref,
    out,
    applied,
    full,
    gram,
    landed,
    summed,
    work,
    inverse_ref,
    mine,
    shares,
    load_sem,
    small_sem,
    store_sem,
    halo_send,
    halo_recv,
    scatter_send,
    scatter_recv,
    gather_send,
    gather_recv,
    share_send,
    share_recv,
):
    points, width = psi_hbm.shape
    me = lax.axis_index("grid")
    cut = lax.axis_index("cuts")
    corner = width // 2
    small_split = width % (2 * lanes) == 0 and (3 * width // 4) % (8 * groups) == 0
    packed = 3 * width // 4 if small_split else width
    parts = (packed // groups, width // groups)
    chunk = lanes * 8
    total_points = points * groups

    steps = points // chunk
    loads = [
        pltpu.make_async_copy(
            psi_hbm.at[pl.ds(i * chunk, chunk)], psi.at[pl.ds(halo + i * chunk, chunk)], load_sem.at[i]
        )
        for i in range(steps)
    ]
    for copy in loads:
        copy.start()
    small = [
        pltpu.make_async_copy(potential_hbm, potential_ref, small_sem.at[0]),
        pltpu.make_async_copy(occupation_hbm, occupation_ref, small_sem.at[1]),
        pltpu.make_async_copy(core_hbm, core_ref, small_sem.at[2]),
    ]
    for copy in small:
        copy.start()
    barrier = pltpu.get_barrier_semaphore()
    for d in range(1, groups):
        pl.semaphore_signal(
            barrier, inc=1, device_id={"grid": lax.rem(me + d, groups)}, device_id_type=pl.DeviceIdType.MESH
        )
    for d in range(1, slices):
        pl.semaphore_signal(
            barrier, inc=1, device_id={"cuts": lax.rem(cut + d, slices)}, device_id_type=pl.DeviceIdType.MESH
        )
    full[...] = jnp.zeros((width, width), jnp.float32)
    gram[1] = jnp.zeros((width, width), jnp.float32)

    for i in range(steps):
        loads[i].wait()
        x = psi[pl.ds(halo + i * chunk, chunk), :]
        full[...] += lax.dot_general(x, x, columns, preferred_element_type=jnp.float32)
    if small_split:
        gram[0, :corner, :] = full[:corner, :]
        gram[0, corner:packed, :corner] = full[corner:packed, corner:]
        gram[0, corner:packed, corner:] = full[packed:, corner:]
    else:
        gram[0] = full[...]
    pl.semaphore_wait(barrier, groups + slices - 2)

    up = pltpu.make_async_remote_copy(
        src_ref=psi_hbm.at[pl.ds(points - halo, halo)],
        dst_ref=psi.at[pl.ds(0, halo)],
        send_sem=halo_send.at[0],
        recv_sem=halo_recv.at[0],
        device_id={"grid": lax.rem(me + 1, groups)},
        device_id_type=pl.DeviceIdType.MESH,
    )
    down = pltpu.make_async_remote_copy(
        src_ref=psi_hbm.at[pl.ds(0, halo)],
        dst_ref=psi.at[pl.ds(points + halo, halo)],
        send_sem=halo_send.at[1],
        recv_sem=halo_recv.at[1],
        device_id={"grid": lax.rem(me + groups - 1, groups)},
        device_id_type=pl.DeviceIdType.MESH,
    )
    up.start()
    down.start()

    def scatter(which):
        part = parts[which]
        copies = []
        for d in range(1, groups):
            to = lax.rem(me + d, groups)
            copies.append(
                pltpu.make_async_remote_copy(
                    src_ref=gram.at[which, pl.ds(pl.multiple_of(to * part, part), part)],
                    dst_ref=landed.at[which, d - 1, pl.ds(0, part)],
                    send_sem=scatter_send.at[which, d - 1],
                    recv_sem=scatter_recv.at[which, d - 1],
                    device_id={"grid": to},
                    device_id_type=pl.DeviceIdType.MESH,
                )
            )
        for copy in copies:
            copy.start()
        return copies

    def gather(which, copies):
        part = parts[which]
        own = pl.ds(pl.multiple_of(me * part, part), part)
        for copy in copies:
            copy.wait()
        total = gram[which, own, :]
        for d in range(groups - 1):
            total = total + landed[which, d, :part, :]
        summed[which, own, :] = total * (1.0 / total_points)
        copies = []
        for d in range(1, groups):
            copies.append(
                pltpu.make_async_remote_copy(
                    src_ref=summed.at[which, own],
                    dst_ref=summed.at[which, own],
                    send_sem=gather_send.at[which, d - 1],
                    recv_sem=gather_recv.at[which, d - 1],
                    device_id={"grid": lax.rem(me + d, groups)},
                    device_id_type=pl.DeviceIdType.MESH,
                )
            )
        for copy in copies:
            copy.start()
        return copies

    first = scatter(0)
    up.wait()
    down.wait()
    for copy in small:
        copy.wait()

    def ritz(i, carry):
        base = pl.multiple_of(i * chunk, chunk)
        values = potential_ref[pl.ds(pl.multiple_of(i * 8, 8), 8), :]
        for s in range(8):
            x = psi[pl.ds(base + s * lanes, lanes + 2 * halo), :].astype(jnp.float32)
            middle = x[halo : halo + lanes]
            before = x[halo - 1 : halo + lanes - 1]
            after = x[halo + 1 : halo + lanes + 1]
            local = jnp.broadcast_to(values[s : s + 1, :], (lanes, lanes)).T
            local = jnp.concatenate([local] * (width // lanes), axis=1)
            kinetic = -0.5 * (after + before - 2.0 * middle)
            applied[s * lanes : (s + 1) * lanes, :] = (kinetic + local * middle).astype(jnp.bfloat16)
        x = psi[pl.ds(base + halo, chunk), :]
        gram[1] += lax.dot_general(x, applied[...], columns, preferred_element_type=jnp.float32)
        return carry

    lax.fori_loop(0, steps // 2, ritz, 0)
    first = gather(0, first)
    lax.fori_loop(steps // 2, steps, ritz, 0)
    second = scatter(1)

    row = lax.broadcasted_iota(jnp.int32, (width, width), 0)
    column = lax.broadcasted_iota(jnp.int32, (width, width), 1)
    identity = (row == column).astype(jnp.float32)
    for copy in first:
        copy.wait()
    if small_split:
        work[:corner, :] = summed[0, :corner, :]
        work[corner:, :corner] = jnp.zeros((width - corner, corner), jnp.float32)
        work[corner:packed, corner:] = summed[0, corner:packed, :corner]
        work[packed:, corner:] = summed[0, corner:packed, corner:]
    else:
        work[...] = summed[0]

    def factor(k, carry):
        here = pl.ds(pl.multiple_of(k * block, block), block)
        rows, own_inverse = eliminate(pltpu.roll(work[here, :], lax.rem(width - k * block, width), 1))
        at = lax.broadcasted_iota(jnp.int32, (block, width), 1)
        wide = jnp.concatenate([own_inverse] * (width // lanes), axis=1)
        solved = pltpu.roll(jnp.where(at < block, wide, rows), k * block, 1)
        ahead = jnp.where(at >= (k + 1) * block, solved, 0.0)
        inverse_ref[here, :] = jnp.where(at >= (k + 1) * block, 0.0, solved)
        ah, am, al = three_parts(ahead)
        sh, sm, sl = three_parts(solved)
        lhs = jnp.concatenate([ah, ah, am, ah, al, am], axis=0)
        rhs = jnp.concatenate([sh, sm, sh, sl, sh, sm], axis=0)
        update = lax.dot_general(lhs, rhs, columns, preferred_element_type=jnp.float32)
        kept = (column < k * block) | (column >= (k + 1) * block)
        work[...] = jnp.where(kept, work[...], 0.0) - update
        return carry

    blocks = width // block
    lax.fori_loop(0, blocks // 2, factor, 0)
    second = gather(1, second)
    lax.fori_loop(blocks // 2, blocks, factor, 0)
    for copy in second:
        copy.wait()

    inverse = inverse_ref[...]
    projected = jnp.dot(inverse, summed[1], precision=highest, preferred_element_type=jnp.float32)
    projected = lax.dot_general(
        projected, inverse, across, precision=highest, preferred_element_type=jnp.float32
    )
    rotation = lax.dot_general(
        inverse,
        identity - step_size * projected,
        columns,
        precision=highest,
        preferred_element_type=jnp.float32,
    ).astype(jnp.bfloat16)

    state = lax.broadcasted_iota(jnp.int32, (1, width), 1)
    live = (state < count_ref[0]).astype(jnp.float32)
    weights = occupation_ref[...].astype(jnp.float32) * live / (2.0 * width * slices)

    stores = []
    for i in range(steps):
        x = psi[pl.ds(halo + i * chunk, chunk), :]
        rotated = jnp.dot(x, rotation, preferred_element_type=jnp.float32)
        out[pl.ds(i * chunk, chunk), :] = rotated.astype(jnp.bfloat16)
        here = pl.ds(i * chunk, chunk)
        stores.append(pltpu.make_async_copy(out.at[here], out_hbm.at[here], store_sem.at[i]))
        stores[i].start()
        square = rotated * rotated * weights
        narrow = square[:, :lanes]
        for c in range(lanes, width, lanes):
            narrow = narrow + square[:, c : c + lanes]
        sums = [
            jnp.sum(narrow[s * lanes : (s + 1) * lanes].T, axis=0, keepdims=True) for s in range(8)
        ]
        mine[i * 8 : (i + 1) * 8, :] = jnp.concatenate(sums, axis=0)
    copies = []
    for d in range(1, slices):
        copies.append(
            pltpu.make_async_remote_copy(
                src_ref=mine,
                dst_ref=shares.at[cut],
                send_sem=share_send.at[d - 1],
                recv_sem=share_recv.at[d - 1],
                device_id={"cuts": lax.rem(cut + d, slices)},
                device_id_type=pl.DeviceIdType.MESH,
            )
        )
    for copy in copies:
        copy.start()
    shares[cut] = mine[...]
    for copy in copies:
        copy.wait()
    density = core_ref[...]
    for c in range(slices):
        density = density + shares[c]
    coefficient = (3.0 / math.pi) ** (1.0 / 3.0)
    root = jnp.exp(jnp.log(density) * (1.0 / 3.0))
    mixed_ref[...] = (1.0 - mixing) * potential_ref[...] + mixing * (-coefficient * root)
    for copy in stores:
        copy.wait()


def per_device(orbitals, potential, core_density, occupation, slice_counts):
    points, width = orbitals.shape
    groups, slices = (lax.axis_size("grid"), lax.axis_size("cuts"))
    folded = (points // lanes, lanes)
    part = width // groups
    steps = points // (8 * lanes)
    hbm = pl.BlockSpec(memory_space=pltpu.HBM)
    orbitals_out, potential_out = pl.pallas_call(
        functools.partial(kernel, groups, slices),
        out_shape=(
            jax.ShapeDtypeStruct((points, width), jnp.bfloat16),
            jax.ShapeDtypeStruct(folded, jnp.float32),
        ),
        in_specs=[hbm, hbm, hbm, hbm, pl.BlockSpec(memory_space=pltpu.SMEM)],
        out_specs=(hbm, pl.BlockSpec(memory_space=pltpu.VMEM)),
        scratch_shapes=[
            pltpu.VMEM((points + 2 * halo, width), jnp.bfloat16),
            pltpu.VMEM(folded, jnp.float32),
            pltpu.VMEM(folded, jnp.float32),
            pltpu.VMEM((1, width), jnp.int32),
            pltpu.VMEM((points, width), jnp.bfloat16),
            pltpu.VMEM((8 * lanes, width), jnp.bfloat16),
            pltpu.VMEM((width, width), jnp.float32),
            pltpu.VMEM((2, width, width), jnp.float32),
            pltpu.VMEM((2, groups - 1, part, width), jnp.float32),
            pltpu.VMEM((2, width, width), jnp.float32),
            pltpu.VMEM((width, width), jnp.float32),
            pltpu.VMEM((width, width), jnp.float32),
            pltpu.VMEM(folded, jnp.float32),
            pltpu.VMEM((slices,) + folded, jnp.float32),
            pltpu.SemaphoreType.DMA((steps,)),
            pltpu.SemaphoreType.DMA((3,)),
            pltpu.SemaphoreType.DMA((steps,)),
            pltpu.SemaphoreType.DMA((2,)),
            pltpu.SemaphoreType.DMA((2,)),
            pltpu.SemaphoreType.DMA((2, groups - 1)),
            pltpu.SemaphoreType.DMA((2, groups - 1)),
            pltpu.SemaphoreType.DMA((2, groups - 1)),
            pltpu.SemaphoreType.DMA((2, groups - 1)),
            pltpu.SemaphoreType.DMA((slices - 1,)),
            pltpu.SemaphoreType.DMA((slices - 1,)),
        ],
        compiler_params=pltpu.CompilerParams(
            collective_id=0, has_side_effects=True, vmem_limit_bytes=60 * 1024 * 1024
        ),
        cost_estimate=pl.CostEstimate(
            flops=8 * points * width * width, bytes_accessed=2 * points * width, transcendentals=0
        ),
    )(
        orbitals,
        potential.reshape(folded),
        core_density.reshape(folded),
        occupation.reshape(1, width),
        slice_counts,
    )
    return (orbitals_out, potential_out.reshape(points))


def solution(mesh):
    placed = (P("grid", "cuts"), P("grid"), P("grid"), P("cuts"), P("cuts"))
    return jax.shard_map(
        per_device,
        mesh=mesh,
        in_specs=placed,
        out_specs=(P("grid", "cuts"), P("grid")),
        check_vma=False,
    )
```

```python
import functools
import math

import jax
import jax.numpy as jnp
from jax import lax
from jax.experimental import pallas as pl
from jax.experimental.pallas import tpu as pltpu
from jax.sharding import PartitionSpec as P

mixing = 0.3
step_size = 0.5
lanes = 128
halo = 16
block = 32
panel = 8
columns = (((0,), (0,)), ((), ()))
across = (((1,), (1,)), ((), ()))
along = (((1,), (0,)), ((), ()))
highest = lax.Precision.HIGHEST


def three_parts(x):
    high = x.astype(jnp.bfloat16)
    rest = x - high.astype(jnp.float32)
    middle = rest.astype(jnp.bfloat16)
    low = (rest - middle.astype(jnp.float32)).astype(jnp.bfloat16)
    return high, middle, low


def spread_rows(tile, r):
    return jnp.broadcast_to(tile[r : r + 1, :], tile.shape)


def eliminate(rows):
    size, width = rows.shape
    shape = (panel, lanes)
    sub = lax.broadcasted_iota(jnp.int32, shape, 0)
    at = lax.broadcasted_iota(jnp.int32, shape, 1)
    count = size // panel
    tiles = []
    for g in range(count):
        group = rows[g * panel : (g + 1) * panel]
        tiles.append([group[:, i : i + lanes] for i in range(0, width, lanes)])
        tiles[g].append((at == sub + g * panel).astype(jnp.float32))
    done = []
    for p in range(count):
        below = range(p + 1, count)
        spread = {
            (g, c): jnp.broadcast_to(tiles[g][0][:, p * panel + c : p * panel + c + 1], shape)
            for g in range(p, count)
            for c in range(panel)
        }
        pivot = {(r, c): spread_rows(spread[p, c], r) for r in range(panel) for c in range(r + 1)}
        lines = [[spread_rows(t, r) for t in tiles[p]] for r in range(panel)]
        factors = {}
        for j in range(panel):
            inverse = pltpu.reciprocal(pivot[j, j], approx=True)
            for r in range(j + 1, panel):
                ratio = pivot[r, j] * inverse
                for c in range(j + 1, r + 1):
                    pivot[r, c] = pivot[r, c] - (pivot[r, j] * pivot[c, j]) * inverse
                lines[r] = [x - ratio * y for x, y in zip(lines[r], lines[j])]
            for g in below:
                factors[g, j] = spread[g, j] * inverse
                for c in range(j + 1, panel):
                    spread[g, c] = spread[g, c] - factors[g, j] * pivot[c, j]
        for g in below:
            for t in range(len(tiles[g])):
                terms = [factors[g, j] * lines[j][t] for j in range(panel)]
                while len(terms) > 1:
                    terms = [x + y for x, y in zip(terms[::2], terms[1::2])]
                tiles[g][t] = tiles[g][t] - terms[0]
        scaled = []
        for r in range(panel):
            root = lax.rsqrt(pivot[r, r])
            scaled.append([x * root for x in lines[r]])
        merged = scaled[0]
        for r in range(1, panel):
            merged = [jnp.where(sub == r, x, y) for x, y in zip(scaled[r], merged)]
        done.append(merged)
    stack = [jnp.concatenate([group[t] for group in done], axis=0) for t in range(len(done[0]))]
    return jnp.concatenate(stack[:-1], axis=1), stack[-1]


def kernel(
    groups,
    slices,
    psi_hbm,
    potential_hbm,
    core_hbm,
    occupation_hbm,
    count_ref,
    out_hbm,
    mixed_ref,
    psi,
    potential_ref,
    core_ref,
    occupation_ref,
    out,
    applied,
    full,
    partial,
    landed,
    summed,
    factors,
    mine,
    shares,
    load_sem,
    small_sem,
    store_sem,
    halo_send,
    halo_recv,
    scatter_send,
    scatter_recv,
    gather_send,
    gather_recv,
    share_send,
    share_recv,
):
    points, width = psi_hbm.shape
    me = lax.axis_index("grid")
    cut = lax.axis_index("cuts")
    chunk = lanes * 8
    total_points = points * groups

    steps = points // chunk
    loads = [
        pltpu.make_async_copy(
            psi_hbm.at[pl.ds(i * chunk, chunk)], psi.at[pl.ds(halo + i * chunk, chunk)], load_sem.at[i]
        )
        for i in range(steps)
    ]
    for copy in loads:
        copy.start()
    small = [
        pltpu.make_async_copy(potential_hbm, potential_ref, small_sem.at[0]),
        pltpu.make_async_copy(occupation_hbm, occupation_ref, small_sem.at[1]),
        pltpu.make_async_copy(core_hbm, core_ref, small_sem.at[2]),
    ]
    for copy in small:
        copy.start()
    barrier = pltpu.get_barrier_semaphore()
    for d in range(1, groups):
        pl.semaphore_signal(
            barrier, inc=1, device_id={"grid": lax.rem(me + d, groups)}, device_id_type=pl.DeviceIdType.MESH
        )
    for d in range(1, slices):
        pl.semaphore_signal(
            barrier, inc=1, device_id={"cuts": lax.rem(cut + d, slices)}, device_id_type=pl.DeviceIdType.MESH
        )
    full[...] = jnp.zeros((width, width), jnp.float32)

    for i in range(steps):
        loads[i].wait()
        x = psi[pl.ds(halo + i * chunk, chunk), :]
        full[...] += lax.dot_general(x, x, columns, preferred_element_type=jnp.float32)
    stages = (
        lambda: full[:lanes, :lanes],
        lambda: jnp.concatenate([full[:lanes, lanes:], full[lanes:, lanes:]], axis=0),
        lambda: full[...],
    )
    pl.semaphore_wait(barrier, groups + slices - 2)

    up = pltpu.make_async_remote_copy(
        src_ref=psi_hbm.at[pl.ds(points - halo, halo)],
        dst_ref=psi.at[pl.ds(0, halo)],
        send_sem=halo_send.at[0],
        recv_sem=halo_recv.at[0],
        device_id={"grid": lax.rem(me + 1, groups)},
        device_id_type=pl.DeviceIdType.MESH,
    )
    down = pltpu.make_async_remote_copy(
        src_ref=psi_hbm.at[pl.ds(0, halo)],
        dst_ref=psi.at[pl.ds(points + halo, halo)],
        send_sem=halo_send.at[1],
        recv_sem=halo_recv.at[1],
        device_id={"grid": lax.rem(me + groups - 1, groups)},
        device_id_type=pl.DeviceIdType.MESH,
    )
    up.start()
    down.start()

    def scatter(which):
        values = stages[which]()
        part = partial[which].shape[1]
        for i in range(groups):
            partial[which][i] = values[i * part : (i + 1) * part]
        copies = []
        for d in range(1, groups):
            to = lax.rem(me + d, groups)
            copies.append(
                pltpu.make_async_remote_copy(
                    src_ref=partial[which].at[to],
                    dst_ref=landed[which].at[d - 1],
                    send_sem=scatter_send.at[which, d - 1],
                    recv_sem=scatter_recv.at[which, d - 1],
                    device_id={"grid": to},
                    device_id_type=pl.DeviceIdType.MESH,
                )
            )
        for copy in copies:
            copy.start()
        return copies

    def gather(which, copies):
        for copy in copies:
            copy.wait()
        total = partial[which][me]
        for d in range(groups - 1):
            total = total + landed[which][d]
        summed[which][me] = total * (1.0 / total_points)
        copies = []
        for d in range(1, groups):
            copies.append(
                pltpu.make_async_remote_copy(
                    src_ref=summed[which].at[me],
                    dst_ref=summed[which].at[me],
                    send_sem=gather_send.at[which, d - 1],
                    recv_sem=gather_recv.at[which, d - 1],
                    device_id={"grid": lax.rem(me + d, groups)},
                    device_id_type=pl.DeviceIdType.MESH,
                )
            )
        for copy in copies:
            copy.start()
        return copies

    def collect(which, copies):
        for copy in copies:
            copy.wait()
        return jnp.concatenate([summed[which][i] for i in range(groups)], axis=0)

    first = scatter(0)
    second = scatter(1)
    up.wait()
    down.wait()
    for copy in small:
        copy.wait()

    def ritz(i, carry):
        base = pl.multiple_of(i * chunk, chunk)
        values = potential_ref[pl.ds(pl.multiple_of(i * 8, 8), 8), :]
        for s in range(8):
            x = psi[pl.ds(base + s * lanes, lanes + 2 * halo), :].astype(jnp.float32)
            middle = x[halo : halo + lanes]
            before = x[halo - 1 : halo + lanes - 1]
            after = x[halo + 1 : halo + lanes + 1]
            local = jnp.broadcast_to(values[s : s + 1, :], (lanes, lanes)).T
            local = jnp.concatenate([local] * (width // lanes), axis=1)
            kinetic = -0.5 * (after + before - 2.0 * middle)
            applied[s * lanes : (s + 1) * lanes, :] = (kinetic + local * middle).astype(jnp.bfloat16)
        x = psi[pl.ds(base + halo, chunk), :]
        full[...] += lax.dot_general(x, applied[...], columns, preferred_element_type=jnp.float32)
        return carry

    full[...] = jnp.zeros((width, width), jnp.float32)
    lax.fori_loop(0, steps // 4, ritz, 0)
    first = gather(0, first)
    lax.fori_loop(steps // 4, steps // 2, ritz, 0)
    second = gather(1, second)
    lax.fori_loop(steps // 2, steps, ritz, 0)
    third = scatter(2)

    at = lax.broadcasted_iota(jnp.int32, (block, lanes), 1)
    column = lax.broadcasted_iota(jnp.int32, (lanes, lanes), 1)

    def factorise(matrix, inverse_ref):
        def factor(k, work):
            rows, own = eliminate(work[:block])
            solved = jnp.where(at < block, own, rows)
            ahead = jnp.where((at >= block) & (at < lanes - k * block), solved, 0.0)
            here = pl.ds(pl.multiple_of(k * block, block), block)
            turned = pltpu.roll(solved, k * block, 1)
            inverse_ref[here, :] = jnp.where(at >= (k + 1) * block, 0.0, turned)
            ah, am, al = three_parts(ahead)
            sh, sm, sl = three_parts(solved)
            lhs = jnp.concatenate([ah, ah, am, ah, al, am], axis=0)
            rhs = jnp.concatenate([sh, sm, sh, sl, sh, sm], axis=0)
            update = lax.dot_general(lhs, rhs, columns, preferred_element_type=jnp.float32)
            work = jnp.where(column < block, 0.0, work) - update
            work = jnp.concatenate([work[block:], work[:block]], axis=0)
            return pltpu.roll(work, lanes - block, 1)

        lax.fori_loop(0, lanes // block, factor, matrix)
        return inverse_ref[...]

    def exact(x, y, contract):
        return lax.dot_general(
            x, y, contract, precision=highest, preferred_element_type=jnp.float32
        )

    lead = factorise(collect(0, first), factors.at[0])
    rest = collect(1, second)
    coupled = exact(lead, rest[:lanes], along)
    third = gather(2, third)
    tail = factorise(rest[lanes:] - exact(coupled, coupled, columns), factors.at[1])
    corner = exact(tail, exact(coupled, lead, columns), along)
    inverse = jnp.concatenate(
        [
            jnp.concatenate([lead, jnp.zeros((lanes, lanes), jnp.float32)], axis=1),
            jnp.concatenate([-corner, tail], axis=1),
        ],
        axis=0,
    )
    ritz_sum = collect(2, third)
    row = lax.broadcasted_iota(jnp.int32, (width, width), 0)
    identity = (row == lax.broadcasted_iota(jnp.int32, (width, width), 1)).astype(jnp.float32)
    projected = exact(exact(inverse, ritz_sum, along), inverse, across)
    rotation = exact(inverse, identity - step_size * projected, columns).astype(jnp.bfloat16)

    state = lax.broadcasted_iota(jnp.int32, (1, width), 1)
    live = (state < count_ref[0]).astype(jnp.float32)
    weights = occupation_ref[...].astype(jnp.float32) * live / (2.0 * width * slices)

    stores = []
    for i in range(steps):
        x = psi[pl.ds(halo + i * chunk, chunk), :]
        rotated = jnp.dot(x, rotation, preferred_element_type=jnp.float32)
        out[pl.ds(i * chunk, chunk), :] = rotated.astype(jnp.bfloat16)
        here = pl.ds(i * chunk, chunk)
        stores.append(pltpu.make_async_copy(out.at[here], out_hbm.at[here], store_sem.at[i]))
        stores[i].start()
        square = rotated * rotated * weights
        narrow = square[:, :lanes]
        for c in range(lanes, width, lanes):
            narrow = narrow + square[:, c : c + lanes]
        sums = [
            jnp.sum(narrow[s * lanes : (s + 1) * lanes].T, axis=0, keepdims=True) for s in range(8)
        ]
        mine[i * 8 : (i + 1) * 8, :] = jnp.concatenate(sums, axis=0)
    copies = []
    for d in range(1, slices):
        copies.append(
            pltpu.make_async_remote_copy(
                src_ref=mine,
                dst_ref=shares.at[cut],
                send_sem=share_send.at[d - 1],
                recv_sem=share_recv.at[d - 1],
                device_id={"cuts": lax.rem(cut + d, slices)},
                device_id_type=pl.DeviceIdType.MESH,
            )
        )
    for copy in copies:
        copy.start()
    shares[cut] = mine[...]
    for copy in copies:
        copy.wait()
    density = core_ref[...]
    for c in range(slices):
        density = density + shares[c]
    coefficient = (3.0 / math.pi) ** (1.0 / 3.0)
    root = jnp.exp(jnp.log(density) * (1.0 / 3.0))
    mixed_ref[...] = (1.0 - mixing) * potential_ref[...] + mixing * (-coefficient * root)
    for copy in stores:
        copy.wait()


def per_device(orbitals, potential, core_density, occupation, slice_counts):
    points, width = orbitals.shape
    groups, slices = (lax.axis_size("grid"), lax.axis_size("cuts"))
    folded = (points // lanes, lanes)
    assert width == 2 * lanes
    parts = [
        (lanes // groups, lanes),
        (width // groups, lanes),
        (width // groups, width),
    ]
    steps = points // (8 * lanes)
    hbm = pl.BlockSpec(memory_space=pltpu.HBM)
    orbitals_out, potential_out = pl.pallas_call(
        functools.partial(kernel, groups, slices),
        out_shape=(
            jax.ShapeDtypeStruct((points, width), jnp.bfloat16),
            jax.ShapeDtypeStruct(folded, jnp.float32),
        ),
        in_specs=[hbm, hbm, hbm, hbm, pl.BlockSpec(memory_space=pltpu.SMEM)],
        out_specs=(hbm, pl.BlockSpec(memory_space=pltpu.VMEM)),
        scratch_shapes=[
            pltpu.VMEM((points + 2 * halo, width), jnp.bfloat16),
            pltpu.VMEM(folded, jnp.float32),
            pltpu.VMEM(folded, jnp.float32),
            pltpu.VMEM((1, width), jnp.int32),
            pltpu.VMEM((points, width), jnp.bfloat16),
            pltpu.VMEM((8 * lanes, width), jnp.bfloat16),
            pltpu.VMEM((width, width), jnp.float32),
            [pltpu.VMEM((groups,) + shape, jnp.float32) for shape in parts],
            [pltpu.VMEM((groups - 1,) + shape, jnp.float32) for shape in parts],
            [pltpu.VMEM((groups,) + shape, jnp.float32) for shape in parts],
            pltpu.VMEM((2, lanes, lanes), jnp.float32),
            pltpu.VMEM(folded, jnp.float32),
            pltpu.VMEM((slices,) + folded, jnp.float32),
            pltpu.SemaphoreType.DMA((steps,)),
            pltpu.SemaphoreType.DMA((3,)),
            pltpu.SemaphoreType.DMA((steps,)),
            pltpu.SemaphoreType.DMA((2,)),
            pltpu.SemaphoreType.DMA((2,)),
            pltpu.SemaphoreType.DMA((3, groups - 1)),
            pltpu.SemaphoreType.DMA((3, groups - 1)),
            pltpu.SemaphoreType.DMA((3, groups - 1)),
            pltpu.SemaphoreType.DMA((3, groups - 1)),
            pltpu.SemaphoreType.DMA((slices - 1,)),
            pltpu.SemaphoreType.DMA((slices - 1,)),
        ],
        compiler_params=pltpu.CompilerParams(
            collective_id=0, has_side_effects=True, vmem_limit_bytes=60 * 1024 * 1024
        ),
        cost_estimate=pl.CostEstimate(
            flops=8 * points * width * width, bytes_accessed=2 * points * width, transcendentals=0
        ),
    )(
        orbitals,
        potential.reshape(folded),
        core_density.reshape(folded),
        occupation.reshape(1, width),
        slice_counts,
    )
    return (orbitals_out, potential_out.reshape(points))


def solution(mesh):
    placed = (P("grid", "cuts"), P("grid"), P("grid"), P("cuts"), P("cuts"))
    return jax.shard_map(
        per_device,
        mesh=mesh,
        in_specs=placed,
        out_specs=(P("grid", "cuts"), P("grid")),
        check_vma=False,
    )
```

```python
import functools
import math

import jax
import jax.numpy as jnp
from jax import lax
from jax.experimental import pallas as pl
from jax.experimental.pallas import tpu as pltpu
from jax.sharding import PartitionSpec as P

mixing = 0.3
step_size = 0.5
lanes = 128
halo = 16
block = 32
panel = 8
columns = (((0,), (0,)), ((), ()))
across = (((1,), (1,)), ((), ()))
along = (((1,), (0,)), ((), ()))
highest = lax.Precision.HIGHEST


def three_parts(x):
    high = x.astype(jnp.bfloat16)
    rest = x - high.astype(jnp.float32)
    middle = rest.astype(jnp.bfloat16)
    low = (rest - middle.astype(jnp.float32)).astype(jnp.bfloat16)
    return high, middle, low


def spread_rows(tile, r):
    return jnp.broadcast_to(tile[r : r + 1, :], tile.shape)


def eliminate(rows):
    size, width = rows.shape
    shape = (panel, lanes)
    sub = lax.broadcasted_iota(jnp.int32, shape, 0)
    at = lax.broadcasted_iota(jnp.int32, shape, 1)
    count = size // panel
    tiles = []
    for g in range(count):
        group = rows[g * panel : (g + 1) * panel]
        tiles.append([group[:, i : i + lanes] for i in range(0, width, lanes)])
        tiles[g].append((at == sub + g * panel).astype(jnp.float32))
    done = []
    for p in range(count):
        below = range(p + 1, count)
        spread = {
            (g, c): jnp.broadcast_to(tiles[g][0][:, p * panel + c : p * panel + c + 1], shape)
            for g in range(p, count)
            for c in range(panel)
        }
        pivot = {(r, c): spread_rows(spread[p, c], r) for r in range(panel) for c in range(r + 1)}
        lines = [[spread_rows(t, r) for t in tiles[p]] for r in range(panel)]
        factors = {}
        for j in range(panel):
            inverse = pltpu.reciprocal(pivot[j, j], approx=True)
            for r in range(j + 1, panel):
                ratio = pivot[r, j] * inverse
                for c in range(j + 1, r + 1):
                    pivot[r, c] = pivot[r, c] - (pivot[r, j] * pivot[c, j]) * inverse
                lines[r] = [x - ratio * y for x, y in zip(lines[r], lines[j])]
            for g in below:
                factors[g, j] = spread[g, j] * inverse
                for c in range(j + 1, panel):
                    spread[g, c] = spread[g, c] - factors[g, j] * pivot[c, j]
        for g in below:
            for t in range(len(tiles[g])):
                terms = [factors[g, j] * lines[j][t] for j in range(panel)]
                while len(terms) > 1:
                    terms = [x + y for x, y in zip(terms[::2], terms[1::2])]
                tiles[g][t] = tiles[g][t] - terms[0]
        scaled = []
        for r in range(panel):
            root = lax.rsqrt(pivot[r, r])
            scaled.append([x * root for x in lines[r]])
        merged = scaled[0]
        for r in range(1, panel):
            merged = [jnp.where(sub == r, x, y) for x, y in zip(scaled[r], merged)]
        done.append(merged)
    stack = [jnp.concatenate([group[t] for group in done], axis=0) for t in range(len(done[0]))]
    return jnp.concatenate(stack[:-1], axis=1), stack[-1]


def kernel(
    groups,
    slices,
    psi_hbm,
    potential_hbm,
    occupation_hbm,
    count_ref,
    rotation_ref,
    density_ref,
    psi,
    potential_ref,
    occupation_ref,
    applied,
    full,
    partial,
    landed,
    summed,
    factors,
    mine,
    shares,
    load_sem,
    small_sem,
    halo_send,
    halo_recv,
    scatter_send,
    scatter_recv,
    gather_send,
    gather_recv,
    share_send,
    share_recv,
):
    points, width = psi_hbm.shape
    me = lax.axis_index("grid")
    cut = lax.axis_index("cuts")
    chunk = lanes * 8
    total_points = points * groups

    steps = points // chunk
    loads = [
        pltpu.make_async_copy(
            psi_hbm.at[pl.ds(i * chunk, chunk)], psi.at[pl.ds(halo + i * chunk, chunk)], load_sem.at[i]
        )
        for i in range(steps)
    ]
    for copy in loads:
        copy.start()
    small = [
        pltpu.make_async_copy(potential_hbm, potential_ref, small_sem.at[0]),
        pltpu.make_async_copy(occupation_hbm, occupation_ref, small_sem.at[1]),
    ]
    for copy in small:
        copy.start()
    barrier = pltpu.get_barrier_semaphore()
    for d in range(1, groups):
        pl.semaphore_signal(
            barrier, inc=1, device_id={"grid": lax.rem(me + d, groups)}, device_id_type=pl.DeviceIdType.MESH
        )
    for d in range(1, slices):
        pl.semaphore_signal(
            barrier, inc=1, device_id={"cuts": lax.rem(cut + d, slices)}, device_id_type=pl.DeviceIdType.MESH
        )
    full[...] = jnp.zeros((width, width), jnp.float32)

    for i in range(steps):
        loads[i].wait()
        x = psi[pl.ds(halo + i * chunk, chunk), :]
        full[...] += lax.dot_general(x, x, columns, preferred_element_type=jnp.float32)
    stages = (
        lambda: full[:lanes, :lanes],
        lambda: jnp.concatenate([full[:lanes, lanes:], full[lanes:, lanes:]], axis=0),
        lambda: full[...],
    )
    pl.semaphore_wait(barrier, groups + slices - 2)

    up = pltpu.make_async_remote_copy(
        src_ref=psi_hbm.at[pl.ds(points - halo, halo)],
        dst_ref=psi.at[pl.ds(0, halo)],
        send_sem=halo_send.at[0],
        recv_sem=halo_recv.at[0],
        device_id={"grid": lax.rem(me + 1, groups)},
        device_id_type=pl.DeviceIdType.MESH,
    )
    down = pltpu.make_async_remote_copy(
        src_ref=psi_hbm.at[pl.ds(0, halo)],
        dst_ref=psi.at[pl.ds(points + halo, halo)],
        send_sem=halo_send.at[1],
        recv_sem=halo_recv.at[1],
        device_id={"grid": lax.rem(me + groups - 1, groups)},
        device_id_type=pl.DeviceIdType.MESH,
    )
    up.start()
    down.start()

    def scatter(which):
        values = stages[which]()
        part = partial[which].shape[1]
        for i in range(groups):
            partial[which][i] = values[i * part : (i + 1) * part]
        copies = []
        for d in range(1, groups):
            to = lax.rem(me + d, groups)
            copies.append(
                pltpu.make_async_remote_copy(
                    src_ref=partial[which].at[to],
                    dst_ref=landed[which].at[d - 1],
                    send_sem=scatter_send.at[which, d - 1],
                    recv_sem=scatter_recv.at[which, d - 1],
                    device_id={"grid": to},
                    device_id_type=pl.DeviceIdType.MESH,
                )
            )
        for copy in copies:
            copy.start()
        return copies

    def gather(which, copies):
        for copy in copies:
            copy.wait()
        total = partial[which][me]
        for d in range(groups - 1):
            total = total + landed[which][d]
        summed[which][me] = total * (1.0 / total_points)
        copies = []
        for d in range(1, groups):
            copies.append(
                pltpu.make_async_remote_copy(
                    src_ref=summed[which].at[me],
                    dst_ref=summed[which].at[me],
                    send_sem=gather_send.at[which, d - 1],
                    recv_sem=gather_recv.at[which, d - 1],
                    device_id={"grid": lax.rem(me + d, groups)},
                    device_id_type=pl.DeviceIdType.MESH,
                )
            )
        for copy in copies:
            copy.start()
        return copies

    def collect(which, copies):
        for copy in copies:
            copy.wait()
        return jnp.concatenate([summed[which][i] for i in range(groups)], axis=0)

    first = scatter(0)
    second = scatter(1)
    up.wait()
    down.wait()
    for copy in small:
        copy.wait()

    def ritz(i, carry):
        base = pl.multiple_of(i * chunk, chunk)
        values = potential_ref[pl.ds(pl.multiple_of(i * 8, 8), 8), :]
        for s in range(8):
            x = psi[pl.ds(base + s * lanes, lanes + 2 * halo), :].astype(jnp.float32)
            middle = x[halo : halo + lanes]
            before = x[halo - 1 : halo + lanes - 1]
            after = x[halo + 1 : halo + lanes + 1]
            local = jnp.broadcast_to(values[s : s + 1, :], (lanes, lanes)).T
            local = jnp.concatenate([local] * (width // lanes), axis=1)
            kinetic = -0.5 * (after + before - 2.0 * middle)
            applied[s * lanes : (s + 1) * lanes, :] = (kinetic + local * middle).astype(jnp.bfloat16)
        x = psi[pl.ds(base + halo, chunk), :]
        full[...] += lax.dot_general(x, applied[...], columns, preferred_element_type=jnp.float32)
        return carry

    full[...] = jnp.zeros((width, width), jnp.float32)
    lax.fori_loop(0, steps // 4, ritz, 0)
    first = gather(0, first)
    lax.fori_loop(steps // 4, steps // 2, ritz, 0)
    second = gather(1, second)
    lax.fori_loop(steps // 2, steps, ritz, 0)
    third = scatter(2)

    at = lax.broadcasted_iota(jnp.int32, (block, lanes), 1)
    column = lax.broadcasted_iota(jnp.int32, (lanes, lanes), 1)

    def factorise(matrix, inverse_ref):
        def factor(k, work):
            rows, own = eliminate(work[:block])
            solved = jnp.where(at < block, own, rows)
            ahead = jnp.where((at >= block) & (at < lanes - k * block), solved, 0.0)
            here = pl.ds(pl.multiple_of(k * block, block), block)
            turned = pltpu.roll(solved, k * block, 1)
            inverse_ref[here, :] = jnp.where(at >= (k + 1) * block, 0.0, turned)
            ah, am, al = three_parts(ahead)
            sh, sm, sl = three_parts(solved)
            lhs = jnp.concatenate([ah, ah, am, ah, al, am], axis=0)
            rhs = jnp.concatenate([sh, sm, sh, sl, sh, sm], axis=0)
            update = lax.dot_general(lhs, rhs, columns, preferred_element_type=jnp.float32)
            work = jnp.where(column < block, 0.0, work) - update
            work = jnp.concatenate([work[block:], work[:block]], axis=0)
            return pltpu.roll(work, lanes - block, 1)

        lax.fori_loop(0, lanes // block, factor, matrix)
        return inverse_ref[...]

    def exact(x, y, contract):
        return lax.dot_general(
            x, y, contract, precision=highest, preferred_element_type=jnp.float32
        )

    lead = factorise(collect(0, first), factors.at[0])
    rest = collect(1, second)
    coupled = exact(lead, rest[:lanes], along)
    third = gather(2, third)
    tail = factorise(rest[lanes:] - exact(coupled, coupled, columns), factors.at[1])
    corner = exact(tail, exact(coupled, lead, columns), along)
    inverse = jnp.concatenate(
        [
            jnp.concatenate([lead, jnp.zeros((lanes, lanes), jnp.float32)], axis=1),
            jnp.concatenate([-corner, tail], axis=1),
        ],
        axis=0,
    )
    ritz_sum = collect(2, third)
    row = lax.broadcasted_iota(jnp.int32, (width, width), 0)
    identity = (row == lax.broadcasted_iota(jnp.int32, (width, width), 1)).astype(jnp.float32)
    projected = exact(exact(inverse, ritz_sum, along), inverse, across)
    rotation = exact(inverse, identity - step_size * projected, columns).astype(jnp.bfloat16)

    state = lax.broadcasted_iota(jnp.int32, (1, width), 1)
    live = (state < count_ref[0]).astype(jnp.float32)
    weights = occupation_ref[...].astype(jnp.float32) * live / (2.0 * width * slices)

    rotation_ref[...] = rotation
    for i in range(steps):
        x = psi[pl.ds(halo + i * chunk, chunk), :]
        rotated = jnp.dot(x, rotation, preferred_element_type=jnp.float32)
        square = rotated * rotated * weights
        narrow = square[:, :lanes]
        for c in range(lanes, width, lanes):
            narrow = narrow + square[:, c : c + lanes]
        sums = [
            jnp.sum(narrow[s * lanes : (s + 1) * lanes].T, axis=0, keepdims=True) for s in range(8)
        ]
        mine[i * 8 : (i + 1) * 8, :] = jnp.concatenate(sums, axis=0)
    copies = []
    for d in range(1, slices):
        copies.append(
            pltpu.make_async_remote_copy(
                src_ref=mine,
                dst_ref=shares.at[cut],
                send_sem=share_send.at[d - 1],
                recv_sem=share_recv.at[d - 1],
                device_id={"cuts": lax.rem(cut + d, slices)},
                device_id_type=pl.DeviceIdType.MESH,
            )
        )
    for copy in copies:
        copy.start()
    shares[cut] = mine[...]
    for copy in copies:
        copy.wait()
    total = shares[0]
    for c in range(1, slices):
        total = total + shares[c]
    density_ref[...] = total


def finish(
    psi_hbm,
    rotation_hbm,
    density_hbm,
    potential_hbm,
    core_hbm,
    out_hbm,
    mixed_ref,
    psi,
    rotation,
    density,
    potential_ref,
    core_ref,
    out,
    load_sem,
    small_sem,
    store_sem,
):
    chunk = 4 * lanes
    pieces = [pl.ds(i * chunk, chunk) for i in range(psi.shape[0] // chunk)]
    first = pltpu.make_async_copy(rotation_hbm, rotation, small_sem.at[0])
    first.start()
    loads = [
        pltpu.make_async_copy(psi_hbm.at[here], psi.at[here], load_sem.at[i])
        for i, here in enumerate(pieces)
    ]
    small = [
        pltpu.make_async_copy(density_hbm, density, small_sem.at[1]),
        pltpu.make_async_copy(potential_hbm, potential_ref, small_sem.at[2]),
        pltpu.make_async_copy(core_hbm, core_ref, small_sem.at[3]),
    ]
    for copy in loads + small:
        copy.start()
    first.wait()
    stores = []
    for i, here in enumerate(pieces):
        loads[i].wait()
        rotated = jnp.dot(psi[here, :], rotation[...], preferred_element_type=jnp.float32)
        out[here, :] = rotated.astype(jnp.bfloat16)
        stores.append(pltpu.make_async_copy(out.at[here], out_hbm.at[here], store_sem.at[i]))
        stores[i].start()
    for copy in small:
        copy.wait()
    coefficient = (3.0 / math.pi) ** (1.0 / 3.0)
    root = jnp.exp(jnp.log(core_ref[...] + density[...]) * (1.0 / 3.0))
    mixed_ref[...] = (1.0 - mixing) * potential_ref[...] + mixing * (-coefficient * root)
    for copy in stores:
        copy.wait()


def per_device(orbitals, potential, core_density, occupation, slice_counts):
    points, width = orbitals.shape
    groups, slices = (lax.axis_size("grid"), lax.axis_size("cuts"))
    folded = (points // lanes, lanes)
    assert width == 2 * lanes
    parts = [
        (lanes // groups, lanes),
        (width // groups, lanes),
        (width // groups, width),
    ]
    steps = points // (8 * lanes)
    hbm = pl.BlockSpec(memory_space=pltpu.HBM)
    vmem = pl.BlockSpec(memory_space=pltpu.VMEM)
    rotation, contribution = pl.pallas_call(
        functools.partial(kernel, groups, slices),
        out_shape=(
            jax.ShapeDtypeStruct((width, width), jnp.bfloat16),
            jax.ShapeDtypeStruct(folded, jnp.float32),
        ),
        in_specs=[hbm, hbm, hbm, pl.BlockSpec(memory_space=pltpu.SMEM)],
        out_specs=(vmem, vmem),
        scratch_shapes=[
            pltpu.VMEM((points + 2 * halo, width), jnp.bfloat16),
            pltpu.VMEM(folded, jnp.float32),
            pltpu.VMEM((1, width), jnp.int32),
            pltpu.VMEM((8 * lanes, width), jnp.bfloat16),
            pltpu.VMEM((width, width), jnp.float32),
            [pltpu.VMEM((groups,) + shape, jnp.float32) for shape in parts],
            [pltpu.VMEM((groups - 1,) + shape, jnp.float32) for shape in parts],
            [pltpu.VMEM((groups,) + shape, jnp.float32) for shape in parts],
            pltpu.VMEM((2, lanes, lanes), jnp.float32),
            pltpu.VMEM(folded, jnp.float32),
            pltpu.VMEM((slices,) + folded, jnp.float32),
            pltpu.SemaphoreType.DMA((steps,)),
            pltpu.SemaphoreType.DMA((2,)),
            pltpu.SemaphoreType.DMA((2,)),
            pltpu.SemaphoreType.DMA((2,)),
            pltpu.SemaphoreType.DMA((3, groups - 1)),
            pltpu.SemaphoreType.DMA((3, groups - 1)),
            pltpu.SemaphoreType.DMA((3, groups - 1)),
            pltpu.SemaphoreType.DMA((3, groups - 1)),
            pltpu.SemaphoreType.DMA((slices - 1,)),
            pltpu.SemaphoreType.DMA((slices - 1,)),
        ],
        compiler_params=pltpu.CompilerParams(
            collective_id=0, has_side_effects=True, vmem_limit_bytes=60 * 1024 * 1024
        ),
        cost_estimate=pl.CostEstimate(
            flops=8 * points * width * width, bytes_accessed=2 * points * width, transcendentals=0
        ),
    )(
        orbitals,
        potential.reshape(folded),
        occupation.reshape(1, width),
        slice_counts,
    )
    orbitals_out, potential_out = pl.pallas_call(
        finish,
        out_shape=(
            jax.ShapeDtypeStruct((points, width), jnp.bfloat16),
            jax.ShapeDtypeStruct(folded, jnp.float32),
        ),
        in_specs=[hbm] * 5,
        out_specs=(hbm, vmem),
        scratch_shapes=[
            pltpu.VMEM((points, width), jnp.bfloat16),
            pltpu.VMEM((width, width), jnp.bfloat16),
            pltpu.VMEM(folded, jnp.float32),
            pltpu.VMEM(folded, jnp.float32),
            pltpu.VMEM(folded, jnp.float32),
            pltpu.VMEM((points, width), jnp.bfloat16),
            pltpu.SemaphoreType.DMA((points // (4 * lanes),)),
            pltpu.SemaphoreType.DMA((4,)),
            pltpu.SemaphoreType.DMA((points // (4 * lanes),)),
        ],
        compiler_params=pltpu.CompilerParams(vmem_limit_bytes=60 * 1024 * 1024),
        cost_estimate=pl.CostEstimate(
            flops=2 * points * width * width, bytes_accessed=4 * points * width, transcendentals=0
        ),
    )(orbitals, rotation, contribution, potential.reshape(folded), core_density.reshape(folded))
    return (orbitals_out, potential_out.reshape(points))


def solution(mesh):
    placed = (P("grid", "cuts"), P("grid"), P("grid"), P("cuts"), P("cuts"))
    return jax.shard_map(
        per_device,
        mesh=mesh,
        in_specs=placed,
        out_specs=(P("grid", "cuts"), P("grid")),
        check_vma=False,
    )
```

```python
import functools
import math

import jax
import jax.numpy as jnp
from jax import lax
from jax.experimental import pallas as pl
from jax.experimental.pallas import tpu as pltpu
from jax.experimental.layout import Layout, with_layout_constraint
from jax.sharding import PartitionSpec as P

mixing = 0.3
step_size = 0.5
lanes = 128
halo = 16
block = 32
panel = 8
columns = (((0,), (0,)), ((), ()))
across = (((1,), (1,)), ((), ()))
along = (((1,), (0,)), ((), ()))
highest = lax.Precision.HIGHEST


def three_parts(x):
    high = x.astype(jnp.bfloat16)
    rest = x - high.astype(jnp.float32)
    middle = rest.astype(jnp.bfloat16)
    low = (rest - middle.astype(jnp.float32)).astype(jnp.bfloat16)
    return high, middle, low


def spread_rows(tile, r):
    return jnp.broadcast_to(tile[r : r + 1, :], tile.shape)


def eliminate(rows):
    size, width = rows.shape
    shape = (panel, lanes)
    sub = lax.broadcasted_iota(jnp.int32, shape, 0)
    at = lax.broadcasted_iota(jnp.int32, shape, 1)
    count = size // panel
    tiles = []
    for g in range(count):
        group = rows[g * panel : (g + 1) * panel]
        tiles.append([group[:, i : i + lanes] for i in range(0, width, lanes)])
        tiles[g].append((at == sub + g * panel).astype(jnp.float32))
    done = []
    for p in range(count):
        below = range(p + 1, count)
        spread = {
            (g, c): jnp.broadcast_to(tiles[g][0][:, p * panel + c : p * panel + c + 1], shape)
            for g in range(p, count)
            for c in range(panel)
        }
        pivot = {(r, c): spread_rows(spread[p, c], r) for r in range(panel) for c in range(r + 1)}
        lines = [[spread_rows(t, r) for t in tiles[p]] for r in range(panel)]
        factors = {}
        for j in range(panel):
            inverse = pltpu.reciprocal(pivot[j, j], approx=True)
            for r in range(j + 1, panel):
                ratio = pivot[r, j] * inverse
                for c in range(j + 1, r + 1):
                    pivot[r, c] = pivot[r, c] - (pivot[r, j] * pivot[c, j]) * inverse
                lines[r] = [x - ratio * y for x, y in zip(lines[r], lines[j])]
            for g in below:
                factors[g, j] = spread[g, j] * inverse
                for c in range(j + 1, panel):
                    spread[g, c] = spread[g, c] - factors[g, j] * pivot[c, j]
        for g in below:
            for t in range(len(tiles[g])):
                terms = [factors[g, j] * lines[j][t] for j in range(panel)]
                while len(terms) > 1:
                    terms = [x + y for x, y in zip(terms[::2], terms[1::2])]
                tiles[g][t] = tiles[g][t] - terms[0]
        scaled = []
        for r in range(panel):
            root = lax.rsqrt(pivot[r, r])
            scaled.append([x * root for x in lines[r]])
        merged = scaled[0]
        for r in range(1, panel):
            merged = [jnp.where(sub == r, x, y) for x, y in zip(scaled[r], merged)]
        done.append(merged)
    stack = [jnp.concatenate([group[t] for group in done], axis=0) for t in range(len(done[0]))]
    return jnp.concatenate(stack[:-1], axis=1), stack[-1]


def kernel(
    groups,
    slices,
    psi_hbm,
    potential_hbm,
    occupation_hbm,
    count_ref,
    rotation_ref,
    density_ref,
    psi,
    potential_ref,
    occupation_ref,
    applied,
    full,
    partial,
    landed,
    summed,
    factors,
    mine,
    shares,
    load_sem,
    small_sem,
    halo_send,
    halo_recv,
    scatter_send,
    scatter_recv,
    gather_send,
    gather_recv,
    share_send,
    share_recv,
):
    points, width = psi_hbm.shape
    me = lax.axis_index("grid")
    cut = lax.axis_index("cuts")
    chunk = lanes * 8
    total_points = points * groups

    steps = points // chunk
    loads = [
        pltpu.make_async_copy(
            psi_hbm.at[pl.ds(i * chunk, chunk)], psi.at[pl.ds(halo + i * chunk, chunk)], load_sem.at[i]
        )
        for i in range(steps)
    ]
    for copy in loads:
        copy.start()
    small = [
        pltpu.make_async_copy(potential_hbm, potential_ref, small_sem.at[0]),
        pltpu.make_async_copy(occupation_hbm, occupation_ref, small_sem.at[1]),
    ]
    for copy in small:
        copy.start()
    barrier = pltpu.get_barrier_semaphore()
    for d in range(1, groups):
        pl.semaphore_signal(
            barrier, inc=1, device_id={"grid": lax.rem(me + d, groups)}, device_id_type=pl.DeviceIdType.MESH
        )
    for d in range(1, slices):
        pl.semaphore_signal(
            barrier, inc=1, device_id={"cuts": lax.rem(cut + d, slices)}, device_id_type=pl.DeviceIdType.MESH
        )
    full[...] = jnp.zeros((width, width), jnp.float32)

    for i in range(steps):
        loads[i].wait()
        x = psi[pl.ds(halo + i * chunk, chunk), :]
        full[...] += lax.dot_general(x, x, columns, preferred_element_type=jnp.float32)
    stages = (
        lambda: full[:lanes, :lanes],
        lambda: jnp.concatenate([full[:lanes, lanes:], full[lanes:, lanes:]], axis=0),
        lambda: full[...],
    )
    pl.semaphore_wait(barrier, groups + slices - 2)

    up = pltpu.make_async_remote_copy(
        src_ref=psi_hbm.at[pl.ds(points - halo, halo)],
        dst_ref=psi.at[pl.ds(0, halo)],
        send_sem=halo_send.at[0],
        recv_sem=halo_recv.at[0],
        device_id={"grid": lax.rem(me + 1, groups)},
        device_id_type=pl.DeviceIdType.MESH,
    )
    down = pltpu.make_async_remote_copy(
        src_ref=psi_hbm.at[pl.ds(0, halo)],
        dst_ref=psi.at[pl.ds(points + halo, halo)],
        send_sem=halo_send.at[1],
        recv_sem=halo_recv.at[1],
        device_id={"grid": lax.rem(me + groups - 1, groups)},
        device_id_type=pl.DeviceIdType.MESH,
    )
    up.start()
    down.start()

    def scatter(which):
        values = stages[which]()
        part = partial[which].shape[1]
        for i in range(groups):
            partial[which][i] = values[i * part : (i + 1) * part]
        copies = []
        for d in range(1, groups):
            to = lax.rem(me + d, groups)
            copies.append(
                pltpu.make_async_remote_copy(
                    src_ref=partial[which].at[to],
                    dst_ref=landed[which].at[d - 1],
                    send_sem=scatter_send.at[which, d - 1],
                    recv_sem=scatter_recv.at[which, d - 1],
                    device_id={"grid": to},
                    device_id_type=pl.DeviceIdType.MESH,
                )
            )
        for copy in copies:
            copy.start()
        return copies

    def gather(which, copies):
        for copy in copies:
            copy.wait()
        total = partial[which][me]
        for d in range(groups - 1):
            total = total + landed[which][d]
        summed[which][me] = total * (1.0 / total_points)
        copies = []
        for d in range(1, groups):
            copies.append(
                pltpu.make_async_remote_copy(
                    src_ref=summed[which].at[me],
                    dst_ref=summed[which].at[me],
                    send_sem=gather_send.at[which, d - 1],
                    recv_sem=gather_recv.at[which, d - 1],
                    device_id={"grid": lax.rem(me + d, groups)},
                    device_id_type=pl.DeviceIdType.MESH,
                )
            )
        for copy in copies:
            copy.start()
        return copies

    def collect(which, copies):
        for copy in copies:
            copy.wait()
        return jnp.concatenate([summed[which][i] for i in range(groups)], axis=0)

    first = scatter(0)
    second = scatter(1)
    up.wait()
    down.wait()
    for copy in small:
        copy.wait()

    def ritz(i, carry):
        base = pl.multiple_of(i * chunk, chunk)
        values = potential_ref[pl.ds(pl.multiple_of(i * 8, 8), 8), :]
        for s in range(8):
            x = psi[pl.ds(base + s * lanes, lanes + 2 * halo), :].astype(jnp.float32)
            middle = x[halo : halo + lanes]
            before = x[halo - 1 : halo + lanes - 1]
            after = x[halo + 1 : halo + lanes + 1]
            local = jnp.broadcast_to(values[s : s + 1, :], (lanes, lanes)).T
            local = jnp.concatenate([local] * (width // lanes), axis=1)
            kinetic = -0.5 * (after + before - 2.0 * middle)
            applied[s * lanes : (s + 1) * lanes, :] = (kinetic + local * middle).astype(jnp.bfloat16)
        x = psi[pl.ds(base + halo, chunk), :]
        full[...] += lax.dot_general(x, applied[...], columns, preferred_element_type=jnp.float32)
        return carry

    full[...] = jnp.zeros((width, width), jnp.float32)
    lax.fori_loop(0, steps // 4, ritz, 0)
    first = gather(0, first)
    lax.fori_loop(steps // 4, steps // 2, ritz, 0)
    second = gather(1, second)
    lax.fori_loop(steps // 2, steps, ritz, 0)
    third = scatter(2)

    at = lax.broadcasted_iota(jnp.int32, (block, lanes), 1)
    column = lax.broadcasted_iota(jnp.int32, (lanes, lanes), 1)

    def factorise(matrix, inverse_ref):
        def factor(k, work):
            rows, own = eliminate(work[:block])
            solved = jnp.where(at < block, own, rows)
            ahead = jnp.where((at >= block) & (at < lanes - k * block), solved, 0.0)
            here = pl.ds(pl.multiple_of(k * block, block), block)
            turned = pltpu.roll(solved, k * block, 1)
            inverse_ref[here, :] = jnp.where(at >= (k + 1) * block, 0.0, turned)
            ah, am, al = three_parts(ahead)
            sh, sm, sl = three_parts(solved)
            lhs = jnp.concatenate([ah, ah, am, ah, al, am], axis=0)
            rhs = jnp.concatenate([sh, sm, sh, sl, sh, sm], axis=0)
            update = lax.dot_general(lhs, rhs, columns, preferred_element_type=jnp.float32)
            work = jnp.where(column < block, 0.0, work) - update
            work = jnp.concatenate([work[block:], work[:block]], axis=0)
            return pltpu.roll(work, lanes - block, 1)

        lax.fori_loop(0, lanes // block, factor, matrix)
        return inverse_ref[...]

    def exact(x, y, contract):
        return lax.dot_general(
            x, y, contract, precision=highest, preferred_element_type=jnp.float32
        )

    lead = factorise(collect(0, first), factors.at[0])
    rest = collect(1, second)
    coupled = exact(lead, rest[:lanes], along)
    third = gather(2, third)
    tail = factorise(rest[lanes:] - exact(coupled, coupled, columns), factors.at[1])
    corner = exact(tail, exact(coupled, lead, columns), along)
    inverse = jnp.concatenate(
        [
            jnp.concatenate([lead, jnp.zeros((lanes, lanes), jnp.float32)], axis=1),
            jnp.concatenate([-corner, tail], axis=1),
        ],
        axis=0,
    )
    ritz_sum = collect(2, third)
    row = lax.broadcasted_iota(jnp.int32, (width, width), 0)
    identity = (row == lax.broadcasted_iota(jnp.int32, (width, width), 1)).astype(jnp.float32)
    projected = exact(exact(inverse, ritz_sum, along), inverse, across)
    rotation = exact(inverse, identity - step_size * projected, columns).astype(jnp.bfloat16)

    state = lax.broadcasted_iota(jnp.int32, (1, width), 1)
    live = (state < count_ref[0]).astype(jnp.float32)
    weights = occupation_ref[...].astype(jnp.float32) * live / (2.0 * width * slices)

    rotation_ref[...] = rotation
    for i in range(steps):
        x = psi[pl.ds(halo + i * chunk, chunk), :]
        rotated = jnp.dot(x, rotation, preferred_element_type=jnp.float32)
        square = rotated * rotated * weights
        narrow = square[:, :lanes]
        for c in range(lanes, width, lanes):
            narrow = narrow + square[:, c : c + lanes]
        sums = [
            jnp.sum(narrow[s * lanes : (s + 1) * lanes].T, axis=0, keepdims=True) for s in range(8)
        ]
        mine[i * 8 : (i + 1) * 8, :] = jnp.concatenate(sums, axis=0)
    copies = []
    for d in range(1, slices):
        copies.append(
            pltpu.make_async_remote_copy(
                src_ref=mine,
                dst_ref=shares.at[cut],
                send_sem=share_send.at[d - 1],
                recv_sem=share_recv.at[d - 1],
                device_id={"cuts": lax.rem(cut + d, slices)},
                device_id_type=pl.DeviceIdType.MESH,
            )
        )
    for copy in copies:
        copy.start()
    shares[cut] = mine[...]
    for copy in copies:
        copy.wait()
    total = shares[0]
    for c in range(1, slices):
        total = total + shares[c]
    density_ref[...] = total


def per_device(orbitals, potential, core_density, occupation, slice_counts):
    points, width = orbitals.shape
    groups, slices = (lax.axis_size("grid"), lax.axis_size("cuts"))
    folded = (points // lanes, lanes)
    assert width == 2 * lanes
    parts = [
        (lanes // groups, lanes),
        (width // groups, lanes),
        (width // groups, width),
    ]
    steps = points // (8 * lanes)
    hbm = pl.BlockSpec(memory_space=pltpu.HBM)
    vmem = pl.BlockSpec(memory_space=pltpu.VMEM)
    rotation, contribution = pl.pallas_call(
        functools.partial(kernel, groups, slices),
        out_shape=(
            jax.ShapeDtypeStruct((width, width), jnp.bfloat16),
            jax.ShapeDtypeStruct(folded, jnp.float32),
        ),
        in_specs=[hbm, hbm, hbm, pl.BlockSpec(memory_space=pltpu.SMEM)],
        out_specs=(vmem, vmem),
        scratch_shapes=[
            pltpu.VMEM((points + 2 * halo, width), jnp.bfloat16),
            pltpu.VMEM(folded, jnp.float32),
            pltpu.VMEM((1, width), jnp.int32),
            pltpu.VMEM((8 * lanes, width), jnp.bfloat16),
            pltpu.VMEM((width, width), jnp.float32),
            [pltpu.VMEM((groups,) + shape, jnp.float32) for shape in parts],
            [pltpu.VMEM((groups - 1,) + shape, jnp.float32) for shape in parts],
            [pltpu.VMEM((groups,) + shape, jnp.float32) for shape in parts],
            pltpu.VMEM((2, lanes, lanes), jnp.float32),
            pltpu.VMEM(folded, jnp.float32),
            pltpu.VMEM((slices,) + folded, jnp.float32),
            pltpu.SemaphoreType.DMA((steps,)),
            pltpu.SemaphoreType.DMA((2,)),
            pltpu.SemaphoreType.DMA((2,)),
            pltpu.SemaphoreType.DMA((2,)),
            pltpu.SemaphoreType.DMA((3, groups - 1)),
            pltpu.SemaphoreType.DMA((3, groups - 1)),
            pltpu.SemaphoreType.DMA((3, groups - 1)),
            pltpu.SemaphoreType.DMA((3, groups - 1)),
            pltpu.SemaphoreType.DMA((slices - 1,)),
            pltpu.SemaphoreType.DMA((slices - 1,)),
        ],
        compiler_params=pltpu.CompilerParams(
            collective_id=0, has_side_effects=True, vmem_limit_bytes=60 * 1024 * 1024
        ),
        cost_estimate=pl.CostEstimate(
            flops=8 * points * width * width, bytes_accessed=2 * points * width, transcendentals=0
        ),
    )(
        orbitals,
        potential.reshape(folded),
        occupation.reshape(1, width),
        slice_counts,
    )
    rotated = jnp.dot(orbitals, rotation, preferred_element_type=jnp.float32)
    rotated = with_layout_constraint(rotated, Layout(major_to_minor=(0, 1)))
    orbitals_out = rotated.astype(jnp.bfloat16)
    coefficient = (3.0 / math.pi) ** (1.0 / 3.0)
    density = core_density + contribution.reshape(points)
    potential_out = (1.0 - mixing) * potential + mixing * (-coefficient * jnp.cbrt(density))
    return (orbitals_out, potential_out)


def solution(mesh):
    placed = (P("grid", "cuts"), P("grid"), P("grid"), P("cuts"), P("cuts"))
    return jax.shard_map(
        per_device,
        mesh=mesh,
        in_specs=placed,
        out_specs=(P("grid", "cuts"), P("grid")),
        check_vma=False,
    )
```

```python
import functools
import math

import jax
import jax.numpy as jnp
from jax import lax
from jax.experimental import pallas as pl
from jax.experimental.pallas import tpu as pltpu
from jax.sharding import PartitionSpec as P

mixing = 0.3
step_size = 0.5
lanes = 128
halo = 16
block = 32
panel = 8
columns = (((0,), (0,)), ((), ()))
across = (((1,), (1,)), ((), ()))
along = (((1,), (0,)), ((), ()))
highest = lax.Precision.HIGHEST


def three_parts(x):
    high = x.astype(jnp.bfloat16)
    rest = x - high.astype(jnp.float32)
    middle = rest.astype(jnp.bfloat16)
    low = (rest - middle.astype(jnp.float32)).astype(jnp.bfloat16)
    return high, middle, low


def spread_rows(tile, r):
    return jnp.broadcast_to(tile[r : r + 1, :], tile.shape)


def eliminate(rows):
    size, width = rows.shape
    shape = (panel, lanes)
    sub = lax.broadcasted_iota(jnp.int32, shape, 0)
    at = lax.broadcasted_iota(jnp.int32, shape, 1)
    count = size // panel
    tiles = []
    for g in range(count):
        group = rows[g * panel : (g + 1) * panel]
        tiles.append([group[:, i : i + lanes] for i in range(0, width, lanes)])
        tiles[g].append((at == sub + g * panel).astype(jnp.float32))
    done = []
    for p in range(count):
        below = range(p + 1, count)
        spread = {
            (g, c): jnp.broadcast_to(tiles[g][0][:, p * panel + c : p * panel + c + 1], shape)
            for g in range(p, count)
            for c in range(panel)
        }
        pivot = {(r, c): spread_rows(spread[p, c], r) for r in range(panel) for c in range(r + 1)}
        lines = [[spread_rows(t, r) for t in tiles[p]] for r in range(panel)]
        factors = {}
        for j in range(panel):
            inverse = pltpu.reciprocal(pivot[j, j], approx=True)
            for r in range(j + 1, panel):
                ratio = pivot[r, j] * inverse
                for c in range(j + 1, r + 1):
                    pivot[r, c] = pivot[r, c] - (pivot[r, j] * pivot[c, j]) * inverse
                lines[r] = [x - ratio * y for x, y in zip(lines[r], lines[j])]
            for g in below:
                factors[g, j] = spread[g, j] * inverse
                for c in range(j + 1, panel):
                    spread[g, c] = spread[g, c] - factors[g, j] * pivot[c, j]
        for g in below:
            for t in range(len(tiles[g])):
                terms = [factors[g, j] * lines[j][t] for j in range(panel)]
                while len(terms) > 1:
                    terms = [x + y for x, y in zip(terms[::2], terms[1::2])]
                tiles[g][t] = tiles[g][t] - terms[0]
        scaled = []
        for r in range(panel):
            root = lax.rsqrt(pivot[r, r])
            scaled.append([x * root for x in lines[r]])
        merged = scaled[0]
        for r in range(1, panel):
            merged = [jnp.where(sub == r, x, y) for x, y in zip(scaled[r], merged)]
        done.append(merged)
    stack = [jnp.concatenate([group[t] for group in done], axis=0) for t in range(len(done[0]))]
    return jnp.concatenate(stack[:-1], axis=1), stack[-1]


def kernel(
    groups,
    slices,
    psi_hbm,
    potential_hbm,
    core_hbm,
    occupation_hbm,
    count_ref,
    out_hbm,
    mixed_ref,
    psi,
    potential_ref,
    core_ref,
    occupation_ref,
    out,
    applied,
    full,
    partial,
    landed,
    summed,
    factors,
    mine,
    shares,
    load_sem,
    small_sem,
    store_sem,
    halo_send,
    halo_recv,
    scatter_send,
    scatter_recv,
    gather_send,
    gather_recv,
    share_send,
    share_recv,
):
    points, width = psi_hbm.shape
    me = lax.axis_index("grid")
    cut = lax.axis_index("cuts")
    chunk = lanes * 8
    total_points = points * groups

    steps = points // chunk
    loads = [
        pltpu.make_async_copy(
            psi_hbm.at[pl.ds(i * chunk, chunk)], psi.at[pl.ds(halo + i * chunk, chunk)], load_sem.at[i]
        )
        for i in range(steps)
    ]
    for copy in loads:
        copy.start()
    small = [
        pltpu.make_async_copy(potential_hbm, potential_ref, small_sem.at[0]),
        pltpu.make_async_copy(occupation_hbm, occupation_ref, small_sem.at[1]),
        pltpu.make_async_copy(core_hbm, core_ref, small_sem.at[2]),
    ]
    for copy in small:
        copy.start()
    barrier = pltpu.get_barrier_semaphore()
    for d in range(1, groups):
        pl.semaphore_signal(
            barrier, inc=1, device_id={"grid": lax.rem(me + d, groups)}, device_id_type=pl.DeviceIdType.MESH
        )
    for d in range(1, slices):
        pl.semaphore_signal(
            barrier, inc=1, device_id={"cuts": lax.rem(cut + d, slices)}, device_id_type=pl.DeviceIdType.MESH
        )
    full[...] = jnp.zeros((width, width), jnp.float32)

    for i in range(steps):
        loads[i].wait()
        x = psi[pl.ds(halo + i * chunk, chunk), :]
        full[...] += lax.dot_general(x, x, columns, preferred_element_type=jnp.float32)
    stages = (
        lambda: full[:lanes, :lanes],
        lambda: jnp.concatenate([full[:lanes, lanes:], full[lanes:, lanes:]], axis=0),
        lambda: full[...],
    )
    pl.semaphore_wait(barrier, groups + slices - 2)

    up = pltpu.make_async_remote_copy(
        src_ref=psi_hbm.at[pl.ds(points - halo, halo)],
        dst_ref=psi.at[pl.ds(0, halo)],
        send_sem=halo_send.at[0],
        recv_sem=halo_recv.at[0],
        device_id={"grid": lax.rem(me + 1, groups)},
        device_id_type=pl.DeviceIdType.MESH,
    )
    down = pltpu.make_async_remote_copy(
        src_ref=psi_hbm.at[pl.ds(0, halo)],
        dst_ref=psi.at[pl.ds(points + halo, halo)],
        send_sem=halo_send.at[1],
        recv_sem=halo_recv.at[1],
        device_id={"grid": lax.rem(me + groups - 1, groups)},
        device_id_type=pl.DeviceIdType.MESH,
    )
    up.start()
    down.start()

    def scatter(which):
        values = stages[which]()
        part = partial[which].shape[1]
        for i in range(groups):
            partial[which][i] = values[i * part : (i + 1) * part]
        copies = []
        for d in range(1, groups):
            to = lax.rem(me + d, groups)
            copies.append(
                pltpu.make_async_remote_copy(
                    src_ref=partial[which].at[to],
                    dst_ref=landed[which].at[d - 1],
                    send_sem=scatter_send.at[which, d - 1],
                    recv_sem=scatter_recv.at[which, d - 1],
                    device_id={"grid": to},
                    device_id_type=pl.DeviceIdType.MESH,
                )
            )
        for copy in copies:
            copy.start()
        return copies

    def gather(which, copies):
        for copy in copies:
            copy.wait()
        total = partial[which][me]
        for d in range(groups - 1):
            total = total + landed[which][d]
        summed[which][me] = total * (1.0 / total_points)
        copies = []
        for d in range(1, groups):
            copies.append(
                pltpu.make_async_remote_copy(
                    src_ref=summed[which].at[me],
                    dst_ref=summed[which].at[me],
                    send_sem=gather_send.at[which, d - 1],
                    recv_sem=gather_recv.at[which, d - 1],
                    device_id={"grid": lax.rem(me + d, groups)},
                    device_id_type=pl.DeviceIdType.MESH,
                )
            )
        for copy in copies:
            copy.start()
        return copies

    def collect(which, copies):
        for copy in copies:
            copy.wait()
        return jnp.concatenate([summed[which][i] for i in range(groups)], axis=0)

    first = scatter(0)
    second = scatter(1)
    up.wait()
    down.wait()
    for copy in small:
        copy.wait()

    def ritz(i, carry):
        base = pl.multiple_of(i * chunk, chunk)
        values = potential_ref[pl.ds(pl.multiple_of(i * 8, 8), 8), :]
        for s in range(8):
            x = psi[pl.ds(base + s * lanes, lanes + 2 * halo), :].astype(jnp.float32)
            middle = x[halo : halo + lanes]
            before = x[halo - 1 : halo + lanes - 1]
            after = x[halo + 1 : halo + lanes + 1]
            local = jnp.broadcast_to(values[s : s + 1, :], (lanes, lanes)).T
            local = jnp.concatenate([local] * (width // lanes), axis=1)
            kinetic = -0.5 * (after + before - 2.0 * middle)
            applied[s * lanes : (s + 1) * lanes, :] = (kinetic + local * middle).astype(jnp.bfloat16)
        x = psi[pl.ds(base + halo, chunk), :]
        full[...] += lax.dot_general(x, applied[...], columns, preferred_element_type=jnp.float32)
        return carry

    full[...] = jnp.zeros((width, width), jnp.float32)
    lax.fori_loop(0, steps // 4, ritz, 0)
    first = gather(0, first)
    lax.fori_loop(steps // 4, steps // 2, ritz, 0)
    second = gather(1, second)
    lax.fori_loop(steps // 2, steps, ritz, 0)
    third = scatter(2)

    at = lax.broadcasted_iota(jnp.int32, (block, lanes), 1)
    column = lax.broadcasted_iota(jnp.int32, (lanes, lanes), 1)

    def factorise(matrix, inverse_ref):
        def factor(k, work):
            rows, own = eliminate(work[:block])
            solved = jnp.where(at < block, own, rows)
            ahead = jnp.where((at >= block) & (at < lanes - k * block), solved, 0.0)
            here = pl.ds(pl.multiple_of(k * block, block), block)
            turned = pltpu.roll(solved, k * block, 1)
            inverse_ref[here, :] = jnp.where(at >= (k + 1) * block, 0.0, turned)
            ah, am, al = three_parts(ahead)
            sh, sm, sl = three_parts(solved)
            lhs = jnp.concatenate([ah, ah, am, ah, al, am], axis=0)
            rhs = jnp.concatenate([sh, sm, sh, sl, sh, sm], axis=0)
            update = lax.dot_general(lhs, rhs, columns, preferred_element_type=jnp.float32)
            work = jnp.where(column < block, 0.0, work) - update
            work = jnp.concatenate([work[block:], work[:block]], axis=0)
            return pltpu.roll(work, lanes - block, 1)

        lax.fori_loop(0, lanes // block, factor, matrix)
        return inverse_ref[...]

    def exact(x, y, contract):
        return lax.dot_general(
            x, y, contract, precision=highest, preferred_element_type=jnp.float32
        )

    lead = factorise(collect(0, first), factors.at[0])
    third = gather(2, third)
    rest = collect(1, second)
    coupled = exact(lead, rest[:lanes], along)
    tail = factorise(rest[lanes:] - exact(coupled, coupled, columns), factors.at[1])
    corner = exact(tail, exact(coupled, lead, columns), along)
    inverse = jnp.concatenate(
        [
            jnp.concatenate([lead, jnp.zeros((lanes, lanes), jnp.float32)], axis=1),
            jnp.concatenate([-corner, tail], axis=1),
        ],
        axis=0,
    )
    ritz_sum = collect(2, third)
    row = lax.broadcasted_iota(jnp.int32, (width, width), 0)
    identity = (row == lax.broadcasted_iota(jnp.int32, (width, width), 1)).astype(jnp.float32)
    projected = exact(exact(inverse, ritz_sum, along), inverse, across)
    rotation = exact(inverse, identity - step_size * projected, columns).astype(jnp.bfloat16)

    state = lax.broadcasted_iota(jnp.int32, (1, width), 1)
    live = (state < count_ref[0]).astype(jnp.float32)
    weights = occupation_ref[...].astype(jnp.float32) * live / (2.0 * width * slices)

    stores = []
    for i in range(steps):
        x = psi[pl.ds(halo + i * chunk, chunk), :]
        rotated = jnp.dot(x, rotation, preferred_element_type=jnp.float32)
        out[pl.ds(i * chunk, chunk), :] = rotated.astype(jnp.bfloat16)
        here = pl.ds(i * chunk, chunk)
        stores.append(pltpu.make_async_copy(out.at[here], out_hbm.at[here], store_sem.at[i]))
        stores[i].start()
        square = rotated * rotated * weights
        narrow = square[:, :lanes]
        for c in range(lanes, width, lanes):
            narrow = narrow + square[:, c : c + lanes]
        sums = [
            jnp.sum(narrow[s * lanes : (s + 1) * lanes].T, axis=0, keepdims=True) for s in range(8)
        ]
        mine[i * 8 : (i + 1) * 8, :] = jnp.concatenate(sums, axis=0)
    copies = []
    for d in range(1, slices):
        copies.append(
            pltpu.make_async_remote_copy(
                src_ref=mine,
                dst_ref=shares.at[cut],
                send_sem=share_send.at[d - 1],
                recv_sem=share_recv.at[d - 1],
                device_id={"cuts": lax.rem(cut + d, slices)},
                device_id_type=pl.DeviceIdType.MESH,
            )
        )
    for copy in copies:
        copy.start()
    shares[cut] = mine[...]
    for copy in copies:
        copy.wait()
    density = core_ref[...]
    for c in range(slices):
        density = density + shares[c]
    coefficient = (3.0 / math.pi) ** (1.0 / 3.0)
    root = jnp.exp(jnp.log(density) * (1.0 / 3.0))
    mixed_ref[...] = (1.0 - mixing) * potential_ref[...] + mixing * (-coefficient * root)
    for copy in stores:
        copy.wait()


def per_device(orbitals, potential, core_density, occupation, slice_counts):
    points, width = orbitals.shape
    groups, slices = (lax.axis_size("grid"), lax.axis_size("cuts"))
    folded = (points // lanes, lanes)
    assert width == 2 * lanes
    parts = [
        (lanes // groups, lanes),
        (width // groups, lanes),
        (width // groups, width),
    ]
    steps = points // (8 * lanes)
    hbm = pl.BlockSpec(memory_space=pltpu.HBM)
    orbitals_out, potential_out = pl.pallas_call(
        functools.partial(kernel, groups, slices),
        out_shape=(
            jax.ShapeDtypeStruct((points, width), jnp.bfloat16),
            jax.ShapeDtypeStruct(folded, jnp.float32),
        ),
        in_specs=[hbm, hbm, hbm, hbm, pl.BlockSpec(memory_space=pltpu.SMEM)],
        out_specs=(hbm, pl.BlockSpec(memory_space=pltpu.VMEM)),
        scratch_shapes=[
            pltpu.VMEM((points + 2 * halo, width), jnp.bfloat16),
            pltpu.VMEM(folded, jnp.float32),
            pltpu.VMEM(folded, jnp.float32),
            pltpu.VMEM((1, width), jnp.int32),
            pltpu.VMEM((points, width), jnp.bfloat16),
            pltpu.VMEM((8 * lanes, width), jnp.bfloat16),
            pltpu.VMEM((width, width), jnp.float32),
            [pltpu.VMEM((groups,) + shape, jnp.float32) for shape in parts],
            [pltpu.VMEM((groups - 1,) + shape, jnp.float32) for shape in parts],
            [pltpu.VMEM((groups,) + shape, jnp.float32) for shape in parts],
            pltpu.VMEM((2, lanes, lanes), jnp.float32),
            pltpu.VMEM(folded, jnp.float32),
            pltpu.VMEM((slices,) + folded, jnp.float32),
            pltpu.SemaphoreType.DMA((steps,)),
            pltpu.SemaphoreType.DMA((3,)),
            pltpu.SemaphoreType.DMA((steps,)),
            pltpu.SemaphoreType.DMA((2,)),
            pltpu.SemaphoreType.DMA((2,)),
            pltpu.SemaphoreType.DMA((3, groups - 1)),
            pltpu.SemaphoreType.DMA((3, groups - 1)),
            pltpu.SemaphoreType.DMA((3, groups - 1)),
            pltpu.SemaphoreType.DMA((3, groups - 1)),
            pltpu.SemaphoreType.DMA((slices - 1,)),
            pltpu.SemaphoreType.DMA((slices - 1,)),
        ],
        compiler_params=pltpu.CompilerParams(
            collective_id=0, has_side_effects=True, vmem_limit_bytes=60 * 1024 * 1024
        ),
        cost_estimate=pl.CostEstimate(
            flops=8 * points * width * width, bytes_accessed=2 * points * width, transcendentals=0
        ),
    )(
        orbitals,
        potential.reshape(folded),
        core_density.reshape(folded),
        occupation.reshape(1, width),
        slice_counts,
    )
    return (orbitals_out, potential_out.reshape(points))


def solution(mesh):
    placed = (P("grid", "cuts"), P("grid"), P("grid"), P("cuts"), P("cuts"))
    return jax.shard_map(
        per_device,
        mesh=mesh,
        in_specs=placed,
        out_specs=(P("grid", "cuts"), P("grid")),
        check_vma=False,
    )
```
